128 devices in a mesh: seq: 16 (over y, z), fsdp: 4 (over x), tp: 2 (over core).
Axes of the slice: x: 4, y: 4, z: 4, core: 2. Of those that a mesh axis runs over, the one named last changes fastest.
Arguments:
- tokens: bfloat16 [8192, 6144], P('seq'), may hold values from -6 to 6
- w_qkv: bfloat16 [6144, 3, 8192], P('seq', None, ('fsdp', 'tp')), may hold values from -0.078125 to 0.078125
- log_decay: float32 [64, 8192], P(('fsdp', 'tp')), may hold values from -1 to 0, as said below
- doc_lengths: int32 [12], replicated, may hold values from 1 to 6144, 8192 in all
- norm_gain: float32 [8192], P(('fsdp', 'tp')), may hold values from 0.25 to 1.75
Outputs:
- attn_out: bfloat16 [8192, 8192], P('seq', ('fsdp', 'tp'))
The draws below stay inside these ranges and needn't reach their ends.
Inputs may be any that keep to these rules, and one draw needn't show every extreme that they name: `doc_lengths`: the lengths of the packed documents in order along the sequence; they sum to 8192. `log_decay`: logarithms of decay factors, all negative.
All inputs are finite; a program needn't handle non-finite values.
Results may differ from the reference program's by a relative error of at most 0.0037.
Values may be sent and summed in bfloat16 or wider, within the bound.
No kernel may reach another device: no remote copies, remote signals or barrier semaphores. Data moves between devices by JAX's collectives and lax.ppermute only.
A program may use at most 128 MiB of HBM per device.

```python
import math
import jax
import jax.numpy as jnp
import numpy as np
from jax import lax

D = 6144
HEADS = 64
HDIM = 128
BLOCK = 256
DOCS = 12
TOK_DEV = 512
LENGTH = 8192


def draw_log_decay(key, part):
    key = jax.random.fold_in(key, 7)
    keys = jax.random.split(key, 6)
    slow_share = 0.5
    slow = jax.random.bernoulli(keys[0], slow_share, (HEADS, 1))
    slow_rate = jnp.exp(jax.random.uniform(keys[1], (HEADS, 1), jnp.float32, math.log(0.2 / LENGTH), math.log(2.0 / LENGTH)))
    fast_rate = jnp.exp(jax.random.uniform(keys[2], (HEADS, 1), jnp.float32, math.log(1.0 / 60.0), math.log(1.0 / 25.0)))
    rate = jnp.where(slow, slow_rate, fast_rate)
    rough = jnp.exp(jax.random.uniform(keys[3], (HEADS, LENGTH), jnp.float32, -0.8, 0.8))
    spots = jax.random.randint(keys[4], (6,), 0, LENGTH)
    struck = jnp.any(jnp.arange(LENGTH)[:, None] == spots[None, :], axis=1)
    loss = jax.random.uniform(keys[5], (HEADS, 1), jnp.float32, 0.22, 0.69)
    return -(rate * rough) - jnp.where(struck[None, :], loss, 0.0)


def shard_levels(own_key, dims, cuts, smallest, top_value):
    loudness = 1.0
    for dim, parts in cuts:
        draws = jax.random.uniform(jax.random.fold_in(jax.random.fold_in(own_key, 6), dim), (parts,), jnp.float32, smallest / len(cuts), top_value / len(cuts))
        loudness = loudness * jnp.repeat(jnp.exp(draws), dims[dim] // parts).reshape((-1,) + (1,) * (len(dims) - 1 - dim))
    return loudness


def length_profile(amount, total, most, lean):
    loads = [(1 << 20) // math.isqrt(standing ** lean) + 1 for standing in range(2, amount + 1)]
    rest, given = total - most - (amount - 1), [1] * (amount - 1)
    while rest > 0:
        free = [i for i in range(amount - 1) if given[i] < most]
        whole, remaining = sum([loads[i] for i in free]), rest
        for i in free:
            extra = min(most - given[i], max(1, remaining * loads[i] // whole), rest)
            given[i] = given[i] + extra
            rest = rest - extra
    return np.array([most] + given)


def uneven_parts(key, amount, total, bound, lean):
    if amount == 2:
        one = jax.random.randint(key, (), max(1, total - bound), min(bound, total - 1) + 1)
        return jnp.stack([one, total - one])
    sizes = jnp.asarray(length_profile(amount, total, bound, lean), jnp.int32)
    couples = (amount - 1) // 2
    donor, receiver = sizes[1:1 + 2 * couples:2], sizes[2:2 + 2 * couples:2]
    slack = jnp.minimum(donor - 1, bound - receiver)
    shifted = jax.random.randint(jax.random.fold_in(key, 1), (couples,), 0, 1 << 20) % (slack + 1)
    sizes = sizes.at[1:1 + 2 * couples:2].set(donor - shifted).at[2:2 + 2 * couples:2].set(receiver + shifted)
    return sizes[jax.random.permutation(jax.random.fold_in(key, 2), amount)]


def scatter_about(own_key, extent, scale, most, cuts=(), held_as=jnp.bfloat16):
    values = scale * jax.random.normal(own_key, extent, jnp.float32)
    if cuts:
        values = values * shard_levels(own_key, extent, cuts, -0.22, 0.18)
    return jnp.clip(values, -most, most).astype(held_as)


def setup_inputs(seed: int = 0) -> dict:
    arg_keys = jax.random.split(jax.random.key(seed), 6)
    return {
        "tokens": scatter_about(arg_keys[0], (LENGTH, D), 1.0, 6.0, ((0, 16),)),
        "w_qkv": scatter_about(arg_keys[1], (D, 3, HEADS * HDIM), D ** -0.5, 0.078125, ((0, 16), (2, 8))),
        "log_decay": draw_log_decay(jax.random.fold_in(arg_keys[5], 71), 0),
        "doc_lengths": uneven_parts(arg_keys[3], DOCS, LENGTH, LENGTH * 3 // 4, 2).astype(jnp.int32),
        "norm_gain": jnp.clip(1.0 + 0.15 * jax.random.normal(arg_keys[4], (HEADS * HDIM,), jnp.float32), 0.25, 1.75),
    }


HIGH = lax.Precision.HIGHEST

def rounded(value):
    return lax.optimization_barrier(value.astype(jnp.bfloat16))

def doc_index(points, ends):
    return lax.optimization_barrier(jnp.sum((points[:, None] >= ends[None, :]).astype(jnp.int32), axis=1))

def local_pass(keys, values, cum, passes, doc, before):
    heads = keys.shape[1]
    blocks = cum.shape[1]
    docb = doc.reshape(blocks, BLOCK)
    lastdoc = docb[:, -1]
    keep = (docb == lastdoc[:, None]).astype(jnp.float32)
    scale = jnp.exp(cum[:, :, -1:] - cum)
    factor = jnp.transpose(scale, (1, 2, 0)) * keep[:, :, None]
    kblock = keys.reshape(blocks, BLOCK, heads, HDIM).astype(jnp.float32)
    vblock = values.reshape(blocks, BLOCK, heads, HDIM).astype(jnp.float32)
    scaled = rounded(kblock * factor[..., None]).astype(jnp.float32)
    kv_block = jnp.einsum('nshe,nshf->nhef', scaled, vblock, precision=HIGH)

    def advance(carried, item):
        local, carry = carried
        block_kv, passing = item
        return ((passing[:, None, None] * local + block_kv, passing * carry), (local, carry))
    start = (jnp.zeros((heads, HDIM, HDIM), jnp.float32), jnp.ones((heads,), jnp.float32))
    ends_state, history = lax.scan(advance, start, (kv_block, passes.T))
    return (history[0], history[1], ends_state[0], ends_state[1])

def second_pass(queries, keys, values, cum, doc, before, local_all, carry_all, incoming):
    heads = keys.shape[1]
    blocks = cum.shape[1]
    docb = doc.reshape(blocks, BLOCK)
    qblock = queries.reshape(blocks, BLOCK, heads, HDIM).astype(jnp.float32)
    kblock = keys.reshape(blocks, BLOCK, heads, HDIM).astype(jnp.float32)
    vblock = values.reshape(blocks, BLOCK, heads, HDIM).astype(jnp.float32)
    scores = jnp.einsum('nthe,nshe->nhts', qblock, kblock, precision=HIGH)
    level = jnp.transpose(cum, (1, 0, 2))
    diff = level[:, :, :, None] - level[:, :, None, :]
    order = jnp.arange(BLOCK, dtype=jnp.int32)
    lower = order[:, None] >= order[None, :]
    same = docb[:, :, None] == docb[:, None, :]
    mask = (lower[None] & same)[:, None]
    weights = rounded(jnp.where(mask, scores * jnp.exp(jnp.where(mask, diff, 0.0)), 0.0))
    intra = jnp.einsum('nhts,nshe->nthe', weights.astype(jnp.float32), vblock, precision=HIGH)
    state = rounded(local_all + carry_all[:, :, None, None] * incoming[None])
    qmask = (docb == before[:, None]).astype(jnp.float32)
    qfactor = jnp.transpose(jnp.exp(level), (0, 2, 1)) * qmask[:, :, None]
    scaled = rounded(qblock * qfactor[..., None])
    inter = jnp.einsum('nthe,nhef->nthf', scaled.astype(jnp.float32), state.astype(jnp.float32), precision=HIGH)
    return (intra + inter).reshape(blocks * BLOCK, heads, HDIM)

def reference(tokens, w_qkv, log_decay, doc_lengths, norm_gain):
    columns = 3 * HEADS * HDIM
    acc = jnp.dot(tokens, w_qkv.reshape(D, columns), preferred_element_type=jnp.float32)
    projected = rounded(jax.nn.silu(acc)).reshape(LENGTH, 3, HEADS, HDIM)
    ends = jnp.cumsum(doc_lengths).astype(jnp.int32)
    every = jnp.arange(LENGTH, dtype=jnp.int32)
    doc_all = doc_index(every, ends)
    prior = jnp.concatenate([jnp.full((1,), -1, jnp.int32), doc_all[:-1]])
    before_all = prior[::BLOCK]
    last_all = doc_all[BLOCK - 1::BLOCK]
    cum_all = jnp.cumsum(log_decay.reshape(HEADS, LENGTH // BLOCK, BLOCK), axis=2)
    pass_all = jnp.where((last_all == before_all)[None, :], jnp.exp(cum_all[:, :, -1]), 0.0)
    spans = LENGTH // TOK_DEV
    blocks = TOK_DEV // BLOCK
    queries = projected[:, 0].reshape(spans, TOK_DEV, HEADS, HDIM)
    keys = projected[:, 1].reshape(spans, TOK_DEV, HEADS, HDIM)
    values = projected[:, 2].reshape(spans, TOK_DEV, HEADS, HDIM)
    cum_x = jnp.transpose(cum_all.reshape(HEADS, spans, blocks, BLOCK), (1, 0, 2, 3))
    pass_x = jnp.transpose(pass_all.reshape(HEADS, spans, blocks), (1, 0, 2))
    doc_x = doc_all.reshape(spans, TOK_DEV)
    before_x = before_all.reshape(spans, blocks)
    gain = norm_gain.reshape(HEADS, HDIM)

    def span_step(incoming, item):
        query, key, value, cum, passes, doc, before = item
        local_all, carry_all, end_local, end_carry = local_pass(key, value, cum, passes, doc, before)
        attended = second_pass(query, key, value, cum, doc, before, local_all, carry_all, incoming)
        squares = lax.optimization_barrier(jnp.sum(attended * attended, axis=(1, 2)))
        scale = lax.rsqrt(squares / (HEADS * HDIM) + 1e-05)
        out = (attended * scale[:, None, None] * gain[None]).astype(jnp.bfloat16)
        span_state = rounded(end_local).astype(jnp.float32)
        return (end_carry[:, None, None] * incoming + span_state, out)
    start = jnp.zeros((HEADS, HDIM, HDIM), jnp.float32)
    _, outs = lax.scan(span_step, start, (queries, keys, values, cum_x, pass_x, doc_x, before_x))
    return outs.reshape(LENGTH, HEADS * HDIM)
```

```python
import functools

import jax
import jax.numpy as jnp
from jax import lax
from jax.experimental import pallas as pl
from jax.experimental.pallas import tpu as pltpu
from jax.sharding import PartitionSpec as P

HEADS = 64
HDIM = 128
BLOCK = 256
SIDE = 4
SPAN = 512
DEPTH = 6144
WROWS = 384
HH = 2
COLS = 3 * HH * HDIM
GROUP = SIDE * SPAN
NB = GROUP // BLOCK
VMEM = pltpu.CompilerParams(vmem_limit_bytes=56 * 1024 * 1024)


def yshift(d):
    return [(s, ((s // 4 + d) % 4) * 4 + s % 4) for s in range(16)]


def zshift(d):
    return [(s, (s // 4) * 4 + (s % 4 + d) % 4) for s in range(16)]


def xshift(d):
    return [(s, (s + d) % 4) for s in range(4)]


def move_y(a, d):
    return lax.ppermute(a, "seq", yshift(d))


def move_z(a, d):
    return lax.ppermute(a, "seq", zshift(d))


def move_x(a, d):
    return lax.ppermute(a, "fsdp", xshift(d))


def swap(a):
    return lax.ppermute(a, "tp", [(0, 1), (1, 0)])


def weight_copies(place, refs, wfull, sem):
    z, y = place[0], place[1]
    groups = [[], [], [], []]
    n = 0
    for k, dz in enumerate((0, 3, 1, 2)):
        zz = lax.rem(z + dz, SIDE)
        for i, (dy, start, rows) in enumerate(
            ((0, 0, 384), (3, 0, 384), (1, 0, 384), (2, 0, 192), (2, 192, 192))
        ):
            yy = lax.rem(y + dy, SIDE)
            at = pl.multiple_of((yy * SIDE + zz) * WROWS + start, 64)
            slot = {0: 0, 3: 1, 1: 2, 2: 3}[dy]
            groups[slot].append(
                pltpu.make_async_copy(refs[5 * k + i], wfull.at[pl.ds(at, rows)], sem.at[n])
            )
            n += 1
    return groups


def half_copies(place, refs, part, half, xbuf, sem, first):
    x, c = place[2], place[3]
    out = []
    for core in range(2):
        g, ap, am, bp, bm = refs[5 * core : 5 * core + 5]
        last = bp if part == 0 else bm
        cc = c if core == 0 else 1 - c
        for dx, ref in ((0, g), (3, ap), (1, am), (2, last)):
            xx = lax.rem(x + dx, SIDE)
            at = pl.multiple_of((xx * 2 + cc) * 64 + half * 32, 32)
            src = ref if dx == 2 else ref.at[pl.ds(32 * part, 32)]
            out.append(
                pltpu.make_async_copy(src, xbuf.at[pl.ds(at, 32)], sem.at[first + len(out)])
            )
    return out


def project_span(place, xbuf, xcopies, wgroups, wfull, acc, result):
    for copy in xcopies:
        copy.wait()
    for i, dy in enumerate((0, 3, 1, 2)):
        if wgroups is not None:
            for copy in wgroups[i]:
                copy.wait()
        yy = lax.rem(place[1] + dy, SIDE)
        at = pl.multiple_of(yy * (SIDE * WROWS), 512)
        part = jnp.dot(
            xbuf[:, pl.ds(at, SIDE * WROWS)],
            wfull[pl.ds(at, SIDE * WROWS), :],
            preferred_element_type=jnp.float32,
        )
        if i == 0:
            acc[...] = part
        else:
            acc[...] += part
    total = acc[...]
    result[...] = (total / (1.0 + jnp.exp(-total))).astype(jnp.bfloat16)


def project_three(place, *refs):
    tokens, g1, g2, w = refs[0], refs[1:11], refs[11:21], refs[21:41]
    out = refs[41]
    xbuf, wfull, acc, result, wsem, xsem, osem = refs[42:]
    wgroups = weight_copies(place, w, wfull, wsem)
    xcopies = [
        [pltpu.make_async_copy(tokens, xbuf.at[0], xsem.at[0])],
        half_copies(place, g1, 0, 0, xbuf.at[1], xsem, 1)
        + half_copies(place, g2, 0, 1, xbuf.at[1], xsem, 9),
        half_copies(place, g1, 1, 1, xbuf.at[2], xsem, 17)
        + half_copies(place, g2, 1, 0, xbuf.at[2], xsem, 25),
    ]
    xcopies[0][0].start()
    for group in wgroups:
        for copy in group:
            copy.start()
    for group in xcopies[1:]:
        for copy in group:
            copy.start()
    outs = []
    for j, dz in enumerate((0, 3, 1)):
        zz = lax.rem(place[0] + dz, SIDE)
        project_span(
            place, xbuf.at[j], xcopies[j], wgroups if j == 0 else None, wfull, acc, result.at[j]
        )
        copy = pltpu.make_async_copy(result.at[j], out.at[zz], osem.at[j])
        copy.start()
        outs.append(copy)
    for copy in outs:
        copy.wait()


def project_last(place, *refs):
    g3, w = refs[0:10], refs[10:30]
    out = refs[31]
    xbuf, wfull, acc, result, wsem, xsem, osem = refs[32:]
    wgroups = weight_copies(place, w, wfull, wsem)
    xcopies = half_copies(place, g3, 0, 0, xbuf, xsem, 0) + half_copies(
        place, g3, 1, 1, xbuf, xsem, 8
    )
    for copy in xcopies:
        copy.start()
    for group in wgroups:
        for copy in group:
            copy.start()
    project_span(place, xbuf, xcopies, wgroups, wfull, acc, result)
    copy = pltpu.make_async_copy(result, out.at[lax.rem(place[0] + 2, SIDE)], osem.at[0])
    copy.start()
    copy.wait()


def call_project(place, tokens, g1, g2, g3, w):
    smem = pl.BlockSpec(memory_space=pltpu.SMEM)
    hbm = pl.BlockSpec(memory_space=pl.ANY)
    flops = 2 * SPAN * DEPTH * COLS
    shape = jax.ShapeDtypeStruct((SIDE, SPAN, COLS), jnp.bfloat16)
    first = pl.pallas_call(
        project_three,
        out_shape=shape,
        in_specs=[smem] + [hbm] * 41,
        out_specs=hbm,
        scratch_shapes=[
            pltpu.VMEM((3, SPAN, DEPTH), jnp.bfloat16),
            pltpu.VMEM((DEPTH, COLS), jnp.bfloat16),
            pltpu.VMEM((SPAN, COLS), jnp.float32),
            pltpu.VMEM((3, SPAN, COLS), jnp.bfloat16),
            pltpu.SemaphoreType.DMA((20,)),
            pltpu.SemaphoreType.DMA((33,)),
            pltpu.SemaphoreType.DMA((3,)),
        ],
        cost_estimate=pl.CostEstimate(flops=3 * flops, bytes_accessed=28 << 20, transcendentals=0),
        compiler_params=VMEM,
        name="project_three",
    )(place, tokens, *g1, *g2, *w)
    return pl.pallas_call(
        project_last,
        out_shape=shape,
        in_specs=[smem] + [hbm] * 31,
        out_specs=hbm,
        scratch_shapes=[
            pltpu.VMEM((SPAN, DEPTH), jnp.bfloat16),
            pltpu.VMEM((DEPTH, COLS), jnp.bfloat16),
            pltpu.VMEM((SPAN, COLS), jnp.float32),
            pltpu.VMEM((SPAN, COLS), jnp.bfloat16),
            pltpu.SemaphoreType.DMA((20,)),
            pltpu.SemaphoreType.DMA((16,)),
            pltpu.SemaphoreType.DMA((1,)),
        ],
        input_output_aliases={31: 0},
        cost_estimate=pl.CostEstimate(flops=flops, bytes_accessed=16 << 20, transcendentals=0),
        compiler_params=VMEM,
        name="project_last",
    )(place, *g3, *w, first)


def states(proj, kf, passes, local, final):
    for h in range(HH):
        held = jnp.zeros((HDIM, HDIM), jnp.float32)
        for b in range(NB):
            rows = pl.ds(b * BLOCK, BLOCK)
            k = proj[rows, pl.ds((HH + h) * HDIM, HDIM)].astype(jnp.float32)
            v = proj[rows, pl.ds((2 * HH + h) * HDIM, HDIM)]
            kd = (k * kf[rows, pl.ds(h, 1)]).astype(jnp.bfloat16)
            kv = lax.dot_general(
                kd, v, (((0,), (0,)), ((), ())), preferred_element_type=jnp.float32
            )
            local[h, b] = held
            held = passes[h, b] * held + kv
        final[h] = held.astype(jnp.bfloat16)


def intras(proj, cumr, cumc, docr, docc, out):
    row = lax.broadcasted_iota(jnp.int32, (BLOCK, BLOCK), 0)
    col = lax.broadcasted_iota(jnp.int32, (BLOCK, BLOCK), 1)
    lower = row >= col
    for b in range(NB):
        rows = pl.ds(b * BLOCK, BLOCK)
        mask = lower & (docc[rows, :] == docr[pl.ds(b, 1), :])
        for h in range(HH):
            q = proj[rows, pl.ds(h * HDIM, HDIM)]
            k = proj[rows, pl.ds((HH + h) * HDIM, HDIM)]
            v = proj[rows, pl.ds((2 * HH + h) * HDIM, HDIM)]
            scores = lax.dot_general(
                q, k, (((1,), (1,)), ((), ())), preferred_element_type=jnp.float32
            )
            diff = cumc[rows, pl.ds(h, 1)] - cumr[h, pl.ds(b, 1), :]
            decay = jnp.exp(jnp.where(mask, diff, 0.0))
            weights = jnp.where(mask, scores * decay, 0.0).astype(jnp.bfloat16)
            out[rows, pl.ds(h * HDIM, HDIM)] = jnp.dot(
                weights, v, preferred_element_type=jnp.float32
            )


def inters(proj, qf, carry, fac, local, s1, s2, s3, intra, out, squares):
    ones = jnp.ones((8, HDIM), jnp.float32)
    for b in range(NB):
        rows = pl.ds(b * BLOCK, BLOCK)
        total = jnp.zeros((8, BLOCK), jnp.float32)
        for h in range(HH):
            incoming = (
                fac[h, 0] * s1[h].astype(jnp.float32)
                + fac[h, 1] * s2[h].astype(jnp.float32)
                + fac[h, 2] * s3[h].astype(jnp.float32)
            )
            state = (local[h, b] + carry[h, b] * incoming).astype(jnp.bfloat16)
            q = proj[rows, pl.ds(h * HDIM, HDIM)].astype(jnp.float32)
            qd = (q * qf[rows, pl.ds(h, 1)]).astype(jnp.bfloat16)
            att = intra[rows, pl.ds(h * HDIM, HDIM)] + jnp.dot(
                qd, state, preferred_element_type=jnp.float32
            )
            total += lax.dot_general(
                ones,
                att * att,
                (((1,), (1,)), ((), ())),
                precision=lax.Precision.HIGHEST,
                preferred_element_type=jnp.float32,
            )
            out[rows, pl.ds(h * HDIM, HDIM)] = att.astype(jnp.bfloat16)
        squares[pl.ds(b, 1), :] = total[0:1, :]


def finish(place, total, gain, p0, p1, p2, p3, out):
    scale = lax.rsqrt(total[...] / (HEADS * HDIM) + 1e-05)
    for b in range(SPAN // BLOCK):
        rows = pl.ds(b * BLOCK, BLOCK)
        column = jnp.transpose(jnp.broadcast_to(scale[b : b + 1, :], (8, BLOCK)))[:, 0:1]
        for dz, piece in ((0, p0), (3, p1), (1, p2), (2, p3)):
            zz = lax.rem(place[0] + dz, SIDE)
            cols = pl.ds(pl.multiple_of(zz * (HH * HDIM), HH * HDIM), HH * HDIM)
            value = piece[rows, :].astype(jnp.float32) * column
            out[rows, cols] = (value * gain[0:1, cols]).astype(jnp.bfloat16)


def ring_x(g):
    ap, am = move_x(g, 1), move_x(g, -1)
    bp, bm = move_x(ap[:32], 1), move_x(am[32:], -1)
    mine = (g, ap, am, bp, bm)
    return mine + tuple(swap(a) for a in mine)


def ring_y(w):
    ap, am = move_y(w, 1), move_y(w, -1)
    bp, bm = move_y(ap[:192], 1), move_y(am[192:], -1)
    return (w, ap, am, bp, bm)


def doc_of(points, ends):
    found = jnp.sum((points[..., None] >= ends).astype(jnp.int32), axis=-1)
    return jnp.where(points < 0, -1, found)


def per_device(tokens, w_qkv, log_decay, doc_lengths, norm_gain):
    here = lax.axis_index("seq")
    y, z = here // SIDE, here % SIDE
    x, c = lax.axis_index("fsdp"), lax.axis_index("tp")
    place = jnp.stack([z, y, x, c]).astype(jnp.int32)

    mine = (2 * x + c) * 64
    lo = lax.dynamic_slice(tokens, (mine, 0), (32, DEPTH))
    hi = lax.dynamic_slice(tokens, (mine + 32, 0), (32, DEPTH))
    m1, p1 = move_z(lo, 1), move_z(hi, -1)
    m2, p2 = move_z(hi, 1), move_z(lo, -1)
    m3, p3 = move_z(m1, 1), move_z(p1, -1)
    g1 = ring_x(jnp.concatenate([m1, p1]))
    g2 = ring_x(jnp.concatenate([m2, p2]))
    g3 = ring_x(jnp.concatenate([m3, p3]))

    wview = w_qkv.reshape(WROWS, 3, SIDE, HH * HDIM)

    def piece(d):
        at = (z + d) % SIDE
        return lax.dynamic_slice(wview, (0, 0, at, 0), (WROWS, 3, 1, HH * HDIM)).reshape(
            WROWS, COLS
        )

    w = []
    for k, d in enumerate((0, 1, -1, 2)):
        part = piece(d % SIDE)
        w += list(ring_y(part if d == 0 else move_z(part, d)))

    ends = jnp.cumsum(doc_lengths)
    nblocks = GROUP * SIDE // BLOCK
    decays = lax.dynamic_slice(log_decay, (HH * z, 0), (HH, GROUP * SIDE))
    cum_all = jnp.cumsum(decays.reshape(HH, nblocks, BLOCK), axis=2)
    starts = jnp.arange(nblocks, dtype=jnp.int32) * BLOCK
    before_all = doc_of(starts - 1, ends)
    last_all = doc_of(starts + (BLOCK - 1), ends)
    pass_all = jnp.where((before_all == last_all)[None], jnp.exp(cum_all[:, :, -1]), 0.0)
    gpass = jnp.prod(pass_all.reshape(HH, SIDE, NB), axis=2)
    f1 = jnp.where(y >= 1, 1.0, 0.0) * jnp.ones((HH,), jnp.float32)
    prev1 = lax.dynamic_index_in_dim(gpass, jnp.maximum(y - 1, 0), 1, keepdims=False)
    prev2 = lax.dynamic_index_in_dim(gpass, jnp.maximum(y - 2, 0), 1, keepdims=False)
    f2 = jnp.where(y >= 2, prev1, 0.0)
    f3 = jnp.where(y >= 3, prev1 * prev2, 0.0)
    fac = jnp.stack([f1, f2, f3], axis=1)
    passes = lax.dynamic_slice_in_dim(pass_all, NB * y, NB, 1)
    carry = jnp.concatenate(
        [jnp.ones((HH, 1), jnp.float32), jnp.cumprod(passes, axis=1)[:, :-1]], axis=1
    )
    cum = lax.dynamic_slice_in_dim(cum_all, NB * y, NB, 1)
    before = lax.dynamic_slice_in_dim(before_all, NB * y, NB, 0)
    last = lax.dynamic_slice_in_dim(last_all, NB * y, NB, 0)
    points = GROUP * y + jnp.arange(GROUP, dtype=jnp.int32).reshape(NB, BLOCK)
    doc = doc_of(points, ends)
    qfac = jnp.where((doc == before[:, None])[None], jnp.exp(cum), 0.0)
    kfac = jnp.where((doc == last[:, None])[None], jnp.exp(cum[:, :, -1:] - cum), 0.0)
    cumc = cum.reshape(HH, GROUP).T
    qf = qfac.reshape(HH, GROUP).T
    kf = kfac.reshape(HH, GROUP).T
    docc = doc.reshape(GROUP, 1)

    proj = call_project(place, tokens, g1, g2, g3, w).reshape(GROUP, COLS)

    smem = pl.BlockSpec(memory_space=pltpu.SMEM)
    vmem = pl.BlockSpec(memory_space=pltpu.VMEM)
    square = (HDIM, HDIM)
    local, final = pl.pallas_call(
        states,
        out_shape=(
            jax.ShapeDtypeStruct((HH, NB) + square, jnp.float32),
            jax.ShapeDtypeStruct((HH,) + square, jnp.bfloat16),
        ),
        in_specs=[vmem, vmem, smem],
        out_specs=(vmem, vmem),
        cost_estimate=pl.CostEstimate(flops=1 << 27, bytes_accessed=4 << 20, transcendentals=0),
        compiler_params=VMEM,
        name="states",
    )(proj, kf, passes)
    s1, s2, s3 = move_y(final, 1), move_y(final, 2), move_y(final, 3)
    intra = pl.pallas_call(
        intras,
        out_shape=jax.ShapeDtypeStruct((GROUP, HH * HDIM), jnp.float32),
        in_specs=[vmem] * 5,
        out_specs=vmem,
        cost_estimate=pl.CostEstimate(flops=1 << 30, bytes_accessed=8 << 20, transcendentals=1 << 20),
        compiler_params=VMEM,
        name="intras",
    )(proj, cum, cumc, doc, docc)
    att, squares = pl.pallas_call(
        inters,
        out_shape=(
            jax.ShapeDtypeStruct((GROUP, HH * HDIM), jnp.bfloat16),
            jax.ShapeDtypeStruct((NB, BLOCK), jnp.float32),
        ),
        in_specs=[vmem, vmem, smem, smem] + [vmem] * 5,
        out_specs=(vmem, vmem),
        cost_estimate=pl.CostEstimate(flops=1 << 28, bytes_accessed=8 << 20, transcendentals=0),
        compiler_params=VMEM,
        name="inters",
    )(proj, qf, carry, fac, local, s1, s2, s3, intra)

    near = SPAN // BLOCK

    def share(a, d, size):
        return lax.dynamic_slice_in_dim(a, ((z + d) % SIDE) * size, size, 0)

    part = share(squares, 0, near)
    for d in (1, -1, 2):
        part = part + move_z(share(squares, d, near), d)
    part = part + swap(part)
    total = part + move_x(part, 1) + move_x(part, -1) + move_x(part, 2)
    pieces = [share(att, 0, SPAN)] + [move_z(share(att, d, SPAN), d) for d in (1, -1, 2)]
    return pl.pallas_call(
        finish,
        out_shape=jax.ShapeDtypeStruct((SPAN, SIDE * HH * HDIM), jnp.bfloat16),
        in_specs=[smem] + [vmem] * 6,
        out_specs=vmem,
        cost_estimate=pl.CostEstimate(flops=1 << 22, bytes_accessed=3 << 20, transcendentals=0),
        compiler_params=VMEM,
        name="finish",
    )(place, total, norm_gain.reshape(1, -1), *pieces)


def solution(mesh):
    in_specs = (
        P("seq", None),
        P("seq", None, ("fsdp", "tp")),
        P(("fsdp", "tp"), None),
        P(),
        P(("fsdp", "tp")),
    )
    out_specs = P("seq", ("fsdp", "tp"))
    return jax.shard_map(
        per_device, mesh=mesh, in_specs=in_specs, out_specs=out_specs, check_vma=False
    )
```

```python
import functools

import jax
import jax.numpy as jnp
from jax import lax
from jax.experimental import pallas as pl
from jax.experimental.pallas import tpu as pltpu
from jax.sharding import PartitionSpec as P

HEADS = 64
HDIM = 128
BLOCK = 256
SIDE = 4
SPAN = 512
DEPTH = 6144
WROWS = 384
HH = 2
COLS = 3 * HH * HDIM
GROUP = SIDE * SPAN
NB = GROUP // BLOCK
VMEM = pltpu.CompilerParams(vmem_limit_bytes=56 * 1024 * 1024)


def zshift(d):
    return [(s, (s // 4) * 4 + (s % 4 + d) % 4) for s in range(16)]


def move_y(a, d):
    perm = [(s, ((s // 4 + d) % 4) * 4 + s % 4) for s in range(16)]
    return lax.ppermute(a, "seq", perm)


def move_z(a, d):
    return lax.ppermute(a, "seq", zshift(d))


def move_x(a, d):
    return lax.ppermute(a, "fsdp", [(s, (s + d) % 4) for s in range(4)])


def swap(a):
    return lax.ppermute(a, "tp", [(0, 1), (1, 0)])


def ring_y(a):
    perm = [
        (2 * s + c, 2 * (((s // 4 + 1 - 2 * c) % 4) * 4 + s % 4) + c)
        for s in range(16)
        for c in range(2)
    ]
    return lax.ppermute(a, ("seq", "tp"), perm)


def ring_z(a, d):
    perm = [
        (2 * s + c, 2 * ((s // 4) * 4 + (s % 4 + d - 2 * d * c) % 4) + c)
        for s in range(16)
        for c in range(2)
    ]
    return lax.ppermute(a, ("seq", "tp"), perm)


def ring_x(a):
    perm = [(2 * s + c, 2 * ((s + 1 - 2 * c) % 4) + c) for s in range(4) for c in range(2)]
    return lax.ppermute(a, ("fsdp", "tp"), perm)


ORDER = (
    "T1 y00 W1 y01:y00 x00:T1 T2:T1 c00:T1 W3:W1 y10:c00 y02:y01 x01:x00 W2:T2 x10:y10 "
    "y30:W3 x02:x01 T3:y02 y20:W2 c02:y30 y31:x10 x20:T3 c01:c02 y21:y20 c03:x02 x11:c01 "
    "y32:y31 c10:c03 x21:x20 c21:y21 y11:c10 c11:c21 y22:y32 x12:x11 c12:c11 y12:y11 "
    "x22:x21 c20:c12 c22:y22 c13:x12 c23:x22"
)


def exchange(tokens, weights):
    got = {"T0": tokens, "W0": weights[0]}
    for item in ORDER.split():
        name, _, after = item.partition(":")
        kind, step = name[0], int(name[-1])
        if kind == "T":
            source = got["T%d" % (step - 1)]
        elif kind == "W":
            source = weights[step]
        elif kind == "y":
            source = got["y" + name[1] + str(step - 1)] if step else got["W" + name[1]]
        elif kind == "x":
            source = got["x" + name[1] + str(step - 1)] if step else got["T%d" % (int(name[1]) + 1)]
        else:
            source = got["x" + name[1] + str(step - 1)] if step else got["T%d" % (int(name[1]) + 1)]
        if after:
            source = lax.optimization_barrier((source, got[after]))[0]
        if kind == "T":
            got[name] = ring_z(source, 1)
        elif kind == "W":
            got[name] = ring_z(source, step)
        elif kind == "y":
            got[name] = ring_y(source)
        elif kind == "x":
            got[name] = ring_x(source)
        else:
            got[name] = swap(source)
    w = [[got["W%d" % k]] + [got["y%d%d" % (k, s)] for s in range(3)] for k in range(4)]
    t = [
        [got["T%d" % (g + 1)]]
        + [got["x%d%d" % (g, s)] for s in range(3)]
        + [got["c%d%d" % (g, s)] for s in range(4)]
        for g in range(3)
    ]
    return t, w


def along(place, axis, steps, up):
    return lax.rem(place[axis] + SIDE + steps * (2 * up - 1), SIDE)


def weight_copies(place, refs, wfull, sem):
    c = place[3]
    groups = []
    for i in range(SIDE):
        yy = along(place, 1, i, c)
        group = []
        for k in range(SIDE):
            zz = along(place, 0, k, c)
            at = pl.multiple_of((yy * SIDE + zz) * WROWS, WROWS)
            n = SIDE * k + i
            group.append(
                pltpu.make_async_copy(refs[n], wfull.at[pl.ds(at, WROWS)], sem.at[n])
            )
        groups.append(group)
    return groups


def token_copies(place, refs, xbuf, sem):
    c = place[3]
    out = []
    for core in range(2):
        cc = c if core == 0 else 1 - c
        for i in range(SIDE):
            n = SIDE * core + i
            xx = along(place, 2, i, cc)
            out.append(pltpu.make_async_copy(refs[n], xbuf.at[cc, xx], sem.at[n]))
    return out


def project(group, place, *refs):
    nx = 1 if group == 0 else 2 * SIDE
    nw = SIDE * SIDE
    xrefs, wrefs = refs[:nx], refs[nx : nx + nw]
    out, xbuf, wfull, acc, result, wsem, xsem, osem = refs[-8:]
    wgroups = weight_copies(place, wrefs, wfull, wsem)
    if group == 0:
        xcopies = [pltpu.make_async_copy(xrefs[0], xbuf, xsem.at[0])]
    else:
        xcopies = token_copies(place, xrefs, xbuf, xsem)
    for copy in xcopies:
        copy.start()
    for wgroup in wgroups:
        for copy in wgroup:
            copy.start()
    for copy in xcopies:
        copy.wait()
    for i in range(SIDE):
        for copy in wgroups[i]:
            copy.wait()
        at = pl.multiple_of(along(place, 1, i, place[3]) * (SIDE * WROWS), SIDE * WROWS)
        x = xbuf[..., pl.ds(at, SIDE * WROWS)].reshape(SPAN, SIDE * WROWS)
        part = jnp.dot(
            x, wfull[pl.ds(at, SIDE * WROWS), :], preferred_element_type=jnp.float32
        )
        if i == 0:
            acc[...] = part
        else:
            acc[...] += part
    total = acc[...]
    total = (total / (1.0 + jnp.exp(-total))).astype(jnp.bfloat16)
    result[...] = total.reshape(result.shape)
    if group == 0:
        copies = [pltpu.make_async_copy(result, out.at[place[0]], osem.at[0])]
    else:
        copies = [
            pltpu.make_async_copy(
                result.at[cc], out.at[along(place, 0, group, cc), :, cc], osem.at[cc]
            )
            for cc in range(2)
        ]
    for copy in copies:
        copy.start()
    for copy in copies:
        copy.wait()


def call_project(place, tokens, groups, w):
    smem = pl.BlockSpec(memory_space=pltpu.SMEM)
    hbm = pl.BlockSpec(memory_space=pl.ANY)
    w = [piece for chunk in w for piece in chunk]
    slices = (SIDE, 2, 64)
    proj = None
    for group, xs in enumerate([[tokens.reshape(slices + (DEPTH,))]] + groups):
        held = [] if proj is None else [proj]
        rows = slices if group == 0 else (2, SIDE, 64)
        proj = pl.pallas_call(
            functools.partial(project, group),
            out_shape=jax.ShapeDtypeStruct((SIDE,) + slices + (COLS,), jnp.bfloat16),
            in_specs=[smem] + [hbm] * (len(xs) + len(w) + len(held)),
            out_specs=hbm,
            scratch_shapes=[
                pltpu.VMEM(rows + (DEPTH,), jnp.bfloat16),
                pltpu.VMEM((DEPTH, COLS), jnp.bfloat16),
                pltpu.VMEM((SPAN, COLS), jnp.float32),
                pltpu.VMEM(rows + (COLS,), jnp.bfloat16),
                pltpu.SemaphoreType.DMA((SIDE * SIDE,)),
                pltpu.SemaphoreType.DMA((2 * SIDE,)),
                pltpu.SemaphoreType.DMA((2,)),
            ],
            input_output_aliases={1 + len(xs) + len(w): 0} if held else {},
            cost_estimate=pl.CostEstimate(
                flops=2 * SPAN * DEPTH * COLS, bytes_accessed=16 << 20, transcendentals=0
            ),
            compiler_params=VMEM,
            name="project%d" % group,
        )(place, *xs, *w, *held)
    return proj


def states(proj, kf, passes, local, final):
    for h in range(HH):
        held = jnp.zeros((HDIM, HDIM), jnp.float32)
        for b in range(NB):
            rows = pl.ds(b * BLOCK, BLOCK)
            k = proj[rows, pl.ds((HH + h) * HDIM, HDIM)].astype(jnp.float32)
            v = proj[rows, pl.ds((2 * HH + h) * HDIM, HDIM)]
            kd = (k * kf[rows, pl.ds(h, 1)]).astype(jnp.bfloat16)
            kv = lax.dot_general(
                kd, v, (((0,), (0,)), ((), ())), preferred_element_type=jnp.float32
            )
            local[h, b] = held
            held = passes[h, b] * held + kv
        final[h] = held.astype(jnp.bfloat16)


def intras(proj, cumr, cumc, docr, docc, out):
    row = lax.broadcasted_iota(jnp.int32, (BLOCK, BLOCK), 0)
    col = lax.broadcasted_iota(jnp.int32, (BLOCK, BLOCK), 1)
    lower = row >= col
    for b in range(NB):
        rows = pl.ds(b * BLOCK, BLOCK)
        mask = lower & (docc[rows, :] == docr[pl.ds(b, 1), :])
        for h in range(HH):
            q = proj[rows, pl.ds(h * HDIM, HDIM)]
            k = proj[rows, pl.ds((HH + h) * HDIM, HDIM)]
            v = proj[rows, pl.ds((2 * HH + h) * HDIM, HDIM)]
            scores = lax.dot_general(
                q, k, (((1,), (1,)), ((), ())), preferred_element_type=jnp.float32
            )
            diff = cumc[rows, pl.ds(h, 1)] - cumr[h, pl.ds(b, 1), :]
            decay = jnp.exp(jnp.where(mask, diff, 0.0))
            weights = jnp.where(mask, scores * decay, 0.0).astype(jnp.bfloat16)
            out[rows, pl.ds(h * HDIM, HDIM)] = jnp.dot(
                weights, v, preferred_element_type=jnp.float32
            )


def inters(proj, qf, carry, fac, local, s1, s2, s3, intra, out, squares):
    ones = jnp.ones((8, HDIM), jnp.float32)
    for b in range(NB):
        rows = pl.ds(b * BLOCK, BLOCK)
        total = jnp.zeros((8, BLOCK), jnp.float32)
        for h in range(HH):
            incoming = (
                fac[h, 0] * s1[h].astype(jnp.float32)
                + fac[h, 1] * s2[h].astype(jnp.float32)
                + fac[h, 2] * s3[h].astype(jnp.float32)
            )
            state = (local[h, b] + carry[h, b] * incoming).astype(jnp.bfloat16)
            q = proj[rows, pl.ds(h * HDIM, HDIM)].astype(jnp.float32)
            qd = (q * qf[rows, pl.ds(h, 1)]).astype(jnp.bfloat16)
            att = intra[rows, pl.ds(h * HDIM, HDIM)] + jnp.dot(
                qd, state, preferred_element_type=jnp.float32
            )
            total += lax.dot_general(
                ones,
                att * att,
                (((1,), (1,)), ((), ())),
                precision=lax.Precision.HIGHEST,
                preferred_element_type=jnp.float32,
            )
            out[rows, pl.ds(h * HDIM, HDIM)] = att.astype(jnp.bfloat16)
        squares[pl.ds(b, 1), :] = total[0:1, :]


def finish(place, total, gain, p0, p1, p2, p3, out):
    scale = lax.rsqrt(total[...] / (HEADS * HDIM) + 1e-05)
    for b in range(SPAN // BLOCK):
        rows = pl.ds(b * BLOCK, BLOCK)
        column = jnp.transpose(jnp.broadcast_to(scale[b : b + 1, :], (8, BLOCK)))[:, 0:1]
        for dz, piece in ((0, p0), (3, p1), (1, p2), (2, p3)):
            zz = lax.rem(place[0] + dz, SIDE)
            cols = pl.ds(pl.multiple_of(zz * (HH * HDIM), HH * HDIM), HH * HDIM)
            value = piece[rows, :].astype(jnp.float32) * column
            out[rows, cols] = (value * gain[0:1, cols]).astype(jnp.bfloat16)


def doc_of(points, ends):
    found = jnp.sum((points[..., None] >= ends).astype(jnp.int32), axis=-1)
    return jnp.where(points < 0, -1, found)


def per_device(tokens, w_qkv, log_decay, doc_lengths, norm_gain):
    here = lax.axis_index("seq")
    y, z = here // SIDE, here % SIDE
    x, c = lax.axis_index("fsdp"), lax.axis_index("tp")
    place = jnp.stack([z, y, x, c]).astype(jnp.int32)

    mine = lax.dynamic_slice(tokens, ((2 * x + c) * 64, 0), (64, DEPTH))
    wview = w_qkv.reshape(WROWS, 3, SIDE, HH * HDIM)
    weights = []
    for d in range(SIDE):
        at = (z + d * (1 - 2 * c)) % SIDE
        weights.append(
            lax.dynamic_slice(wview, (0, 0, at, 0), (WROWS, 3, 1, HH * HDIM)).reshape(WROWS, COLS)
        )
    t, w = exchange(mine, weights)

    ends = jnp.cumsum(doc_lengths)
    nblocks = GROUP * SIDE // BLOCK
    decays = lax.dynamic_slice(log_decay, (HH * z, 0), (HH, GROUP * SIDE))
    cum_all = jnp.cumsum(decays.reshape(HH, nblocks, BLOCK), axis=2)
    starts = jnp.arange(nblocks, dtype=jnp.int32) * BLOCK
    before_all = doc_of(starts - 1, ends)
    last_all = doc_of(starts + (BLOCK - 1), ends)
    pass_all = jnp.where((before_all == last_all)[None], jnp.exp(cum_all[:, :, -1]), 0.0)
    gpass = jnp.prod(pass_all.reshape(HH, SIDE, NB), axis=2)
    f1 = jnp.where(y >= 1, 1.0, 0.0) * jnp.ones((HH,), jnp.float32)
    prev1 = lax.dynamic_index_in_dim(gpass, jnp.maximum(y - 1, 0), 1, keepdims=False)
    prev2 = lax.dynamic_index_in_dim(gpass, jnp.maximum(y - 2, 0), 1, keepdims=False)
    f2 = jnp.where(y >= 2, prev1, 0.0)
    f3 = jnp.where(y >= 3, prev1 * prev2, 0.0)
    fac = jnp.stack([f1, f2, f3], axis=1)
    passes = lax.dynamic_slice_in_dim(pass_all, NB * y, NB, 1)
    carry = jnp.concatenate(
        [jnp.ones((HH, 1), jnp.float32), jnp.cumprod(passes, axis=1)[:, :-1]], axis=1
    )
    cum = lax.dynamic_slice_in_dim(cum_all, NB * y, NB, 1)
    before = lax.dynamic_slice_in_dim(before_all, NB * y, NB, 0)
    last = lax.dynamic_slice_in_dim(last_all, NB * y, NB, 0)
    points = GROUP * y + jnp.arange(GROUP, dtype=jnp.int32).reshape(NB, BLOCK)
    doc = doc_of(points, ends)
    qfac = jnp.where((doc == before[:, None])[None], jnp.exp(cum), 0.0)
    kfac = jnp.where((doc == last[:, None])[None], jnp.exp(cum[:, :, -1:] - cum), 0.0)
    cumc = cum.reshape(HH, GROUP).T
    qf = qfac.reshape(HH, GROUP).T
    kf = kfac.reshape(HH, GROUP).T
    docc = doc.reshape(GROUP, 1)

    proj = call_project(place, tokens, t, w).reshape(GROUP, COLS)

    smem = pl.BlockSpec(memory_space=pltpu.SMEM)
    vmem = pl.BlockSpec(memory_space=pltpu.VMEM)
    square = (HDIM, HDIM)
    local, final = pl.pallas_call(
        states,
        out_shape=(
            jax.ShapeDtypeStruct((HH, NB) + square, jnp.float32),
            jax.ShapeDtypeStruct((HH,) + square, jnp.bfloat16),
        ),
        in_specs=[vmem, vmem, smem],
        out_specs=(vmem, vmem),
        cost_estimate=pl.CostEstimate(flops=1 << 27, bytes_accessed=4 << 20, transcendentals=0),
        compiler_params=VMEM,
        name="states",
    )(proj, kf, passes)
    s1, s2, s3 = move_y(final, 1), move_y(final, 2), move_y(final, 3)
    intra = pl.pallas_call(
        intras,
        out_shape=jax.ShapeDtypeStruct((GROUP, HH * HDIM), jnp.float32),
        in_specs=[vmem] * 5,
        out_specs=vmem,
        cost_estimate=pl.CostEstimate(flops=1 << 30, bytes_accessed=8 << 20, transcendentals=1 << 20),
        compiler_params=VMEM,
        name="intras",
    )(proj, cum, cumc, doc, docc)
    att, squares = pl.pallas_call(
        inters,
        out_shape=(
            jax.ShapeDtypeStruct((GROUP, HH * HDIM), jnp.bfloat16),
            jax.ShapeDtypeStruct((NB, BLOCK), jnp.float32),
        ),
        in_specs=[vmem, vmem, smem, smem] + [vmem] * 5,
        out_specs=(vmem, vmem),
        cost_estimate=pl.CostEstimate(flops=1 << 28, bytes_accessed=8 << 20, transcendentals=0),
        compiler_params=VMEM,
        name="inters",
    )(proj, qf, carry, fac, local, s1, s2, s3, intra)

    near = SPAN // BLOCK

    def share(a, d, size):
        return lax.dynamic_slice_in_dim(a, ((z + d) % SIDE) * size, size, 0)

    part = share(squares, 0, near)
    for d in (1, -1, 2):
        part = part + move_z(share(squares, d, near), d)
    part = part + swap(part)
    total = part + move_x(part, 1) + move_x(part, -1) + move_x(part, 2)
    pieces = [share(att, 0, SPAN)] + [move_z(share(att, d, SPAN), d) for d in (1, -1, 2)]
    return pl.pallas_call(
        finish,
        out_shape=jax.ShapeDtypeStruct((SPAN, SIDE * HH * HDIM), jnp.bfloat16),
        in_specs=[smem] + [vmem] * 6,
        out_specs=vmem,
        cost_estimate=pl.CostEstimate(flops=1 << 22, bytes_accessed=3 << 20, transcendentals=0),
        compiler_params=VMEM,
        name="finish",
    )(place, total, norm_gain.reshape(1, -1), *pieces)


def solution(mesh):
    in_specs = (
        P("seq", None),
        P("seq", None, ("fsdp", "tp")),
        P(("fsdp", "tp"), None),
        P(),
        P(("fsdp", "tp")),
    )
    out_specs = P("seq", ("fsdp", "tp"))
    return jax.shard_map(
        per_device, mesh=mesh, in_specs=in_specs, out_specs=out_specs, check_vma=False
    )
```

```python
import functools

import jax
import jax.numpy as jnp
from jax import lax
from jax.experimental import pallas as pl
from jax.experimental.pallas import tpu as pltpu
from jax.sharding import PartitionSpec as P

AXES = ("y", "z", "x", "c")
HEADS = 64
HDIM = 128
BLOCK = 256
SIDE = 4
SPAN = 512
DEPTH = 6144
WROWS = 384
HH = 2
COLS = 3 * HH * HDIM
GROUP = SIDE * SPAN
NB = GROUP // BLOCK
VMEM = pltpu.CompilerParams(vmem_limit_bytes=56 * 1024 * 1024)


def move_y(a, d):
    return lax.ppermute(a, "y", [(s, (s + d) % 4) for s in range(4)])


def move_z(a, d):
    return lax.ppermute(a, "z", [(s, (s + d) % 4) for s in range(4)])


def move_x(a, d):
    return lax.ppermute(a, "x", [(s, (s + d) % 4) for s in range(4)])


def swap(a):
    return lax.ppermute(a, "c", [(0, 1), (1, 0)])


def opposed(a, axis, d):
    perm = [(2 * s + c, 2 * ((s + d - 2 * d * c) % 4) + c) for s in range(4) for c in range(2)]
    return lax.ppermute(a, (axis, "c"), perm)


def spread_weights(weights):
    out = []
    for k, piece in enumerate(weights):
        row = [opposed(piece, "z", k) if k else piece]
        for _ in range(SIDE - 1):
            row.append(opposed(row[-1], "y", 1))
        out += row
    return out


def along(place, axis, steps):
    return lax.rem(place[axis] + SIDE + steps * (2 * place[3] - 1), SIDE)


def project(spans, place, x, *refs):
    wrefs = refs[: SIDE * SIDE]
    out, wfull, acc, sem = refs[-4:]
    step = pl.program_id(0)

    def copies(i):
        yy = along(place, 1, i)
        for k in range(SIDE):
            at = pl.multiple_of((yy * SIDE + along(place, 0, k)) * WROWS, WROWS)
            n = SIDE * k + i
            yield pltpu.make_async_copy(wrefs[n], wfull.at[pl.ds(at, WROWS)], sem.at[n])

    @pl.when(step == 0)
    def _():
        for i in range(SIDE):
            for copy in copies(i):
                copy.start()

    for i in range(SIDE):

        @pl.when(step == 0)
        def _():
            for copy in copies(i):
                copy.wait()

        at = pl.multiple_of(along(place, 1, i) * (SIDE * WROWS), SIDE * WROWS)
        part = jnp.dot(
            x[:, pl.ds(at, SIDE * WROWS)],
            wfull[pl.ds(at, SIDE * WROWS), :],
            preferred_element_type=jnp.float32,
        )
        if i == 0:
            acc[...] = part
        else:
            acc[...] += part
    total = acc[...]
    out[...] = (total / (1.0 + jnp.exp(-total))).astype(jnp.bfloat16)


def call_project(place, rows, w, held):
    tile = 256
    per = SPAN // tile
    spans = SIDE - 1 if held else 1

    def there(i, place):
        return (lax.rem(place[0] + (i // per + 1 if held else 0), SIDE) * per + i % per, 0)

    def here(i, place):
        return (i, 0)

    hbm = pl.BlockSpec(memory_space=pl.ANY)
    return pl.pallas_call(
        functools.partial(project, spans),
        out_shape=jax.ShapeDtypeStruct((GROUP, COLS), jnp.bfloat16),
        grid_spec=pltpu.PrefetchScalarGridSpec(
            num_scalar_prefetch=1,
            grid=(spans * per,),
            in_specs=[pl.BlockSpec((tile, DEPTH), there if held else here)]
            + [hbm] * (len(w) + len(held)),
            out_specs=pl.BlockSpec((tile, COLS), there),
            scratch_shapes=[
                pltpu.VMEM((DEPTH, COLS), jnp.bfloat16),
                pltpu.VMEM((tile, COLS), jnp.float32),
                pltpu.SemaphoreType.DMA((SIDE * SIDE,)),
            ],
        ),
        input_output_aliases={2 + len(w): 0} if held else {},
        cost_estimate=pl.CostEstimate(
            flops=2 * spans * SPAN * DEPTH * COLS,
            bytes_accessed=(10 + 7 * spans) << 20,
            transcendentals=0,
        ),
        compiler_params=VMEM,
        name="project_others" if held else "project_own",
    )(place, rows, *w, *held)


def states(proj, kf, passes, local, final):
    for h in range(HH):
        held = jnp.zeros((HDIM, HDIM), jnp.float32)
        for b in range(NB):
            rows = pl.ds(b * BLOCK, BLOCK)
            k = proj[rows, pl.ds((HH + h) * HDIM, HDIM)].astype(jnp.float32)
            v = proj[rows, pl.ds((2 * HH + h) * HDIM, HDIM)]
            kd = (k * kf[rows, pl.ds(h, 1)]).astype(jnp.bfloat16)
            kv = lax.dot_general(
                kd, v, (((0,), (0,)), ((), ())), preferred_element_type=jnp.float32
            )
            local[h, b] = held
            held = passes[h, b] * held + kv
        final[h] = held.astype(jnp.bfloat16)


def intras(proj, cumr, cumc, docr, docc, out):
    row = lax.broadcasted_iota(jnp.int32, (BLOCK, BLOCK), 0)
    col = lax.broadcasted_iota(jnp.int32, (BLOCK, BLOCK), 1)
    lower = row >= col
    for b in range(NB):
        rows = pl.ds(b * BLOCK, BLOCK)
        mask = lower & (docc[rows, :] == docr[pl.ds(b, 1), :])
        for h in range(HH):
            q = proj[rows, pl.ds(h * HDIM, HDIM)]
            k = proj[rows, pl.ds((HH + h) * HDIM, HDIM)]
            v = proj[rows, pl.ds((2 * HH + h) * HDIM, HDIM)]
            scores = lax.dot_general(
                q, k, (((1,), (1,)), ((), ())), preferred_element_type=jnp.float32
            )
            diff = cumc[rows, pl.ds(h, 1)] - cumr[h, pl.ds(b, 1), :]
            decay = jnp.exp(jnp.where(mask, diff, 0.0))
            weights = jnp.where(mask, scores * decay, 0.0).astype(jnp.bfloat16)
            out[rows, pl.ds(h * HDIM, HDIM)] = jnp.dot(
                weights, v, preferred_element_type=jnp.float32
            )


def inters(proj, qf, carry, fac, local, s1, s2, s3, intra, out, squares):
    ones = jnp.ones((8, HDIM), jnp.float32)
    for b in range(NB):
        rows = pl.ds(b * BLOCK, BLOCK)
        total = jnp.zeros((8, BLOCK), jnp.float32)
        for h in range(HH):
            incoming = (
                fac[h, 0] * s1[h].astype(jnp.float32)
                + fac[h, 1] * s2[h].astype(jnp.float32)
                + fac[h, 2] * s3[h].astype(jnp.float32)
            )
            state = (local[h, b] + carry[h, b] * incoming).astype(jnp.bfloat16)
            q = proj[rows, pl.ds(h * HDIM, HDIM)].astype(jnp.float32)
            qd = (q * qf[rows, pl.ds(h, 1)]).astype(jnp.bfloat16)
            att = intra[rows, pl.ds(h * HDIM, HDIM)] + jnp.dot(
                qd, state, preferred_element_type=jnp.float32
            )
            total += lax.dot_general(
                ones,
                att * att,
                (((1,), (1,)), ((), ())),
                precision=lax.Precision.HIGHEST,
                preferred_element_type=jnp.float32,
            )
            out[rows, pl.ds(h * HDIM, HDIM)] = att.astype(jnp.bfloat16)
        squares[pl.ds(b, 1), :] = total[0:1, :]


def finish(place, total, gain, p0, p1, p2, p3, out):
    scale = lax.rsqrt(total[...] / (HEADS * HDIM) + 1e-05)
    for b in range(SPAN // BLOCK):
        rows = pl.ds(b * BLOCK, BLOCK)
        column = jnp.transpose(jnp.broadcast_to(scale[b : b + 1, :], (8, BLOCK)))[:, 0:1]
        for dz, piece in ((0, p0), (3, p1), (1, p2), (2, p3)):
            zz = lax.rem(place[0] + dz, SIDE)
            cols = pl.ds(pl.multiple_of(zz * (HH * HDIM), HH * HDIM), HH * HDIM)
            value = piece[rows, :].astype(jnp.float32) * column
            out[rows, cols] = (value * gain[0:1, cols]).astype(jnp.bfloat16)


def doc_of(points, ends):
    found = jnp.sum((points[..., None] >= ends).astype(jnp.int32), axis=-1)
    return jnp.where(points < 0, -1, found)


def per_device(tokens, w_qkv, log_decay, doc_lengths, norm_gain):
    y, z, x, c = [lax.axis_index(axis) for axis in AXES]
    place = jnp.stack([z, y, x, c]).astype(jnp.int32)

    mine = lax.dynamic_slice(tokens, ((2 * x + c) * 64, 0), (64, DEPTH))
    wview = w_qkv.reshape(WROWS, 3, SIDE, HH * HDIM)
    weights = []
    for d in range(SIDE):
        at = (z + d * (1 - 2 * c)) % SIDE
        weights.append(
            lax.dynamic_slice(wview, (0, 0, at, 0), (WROWS, 3, 1, HH * HDIM)).reshape(WROWS, COLS)
        )
    group = lax.all_gather(mine, ("z", "x", "c"), axis=0, tiled=True)
    w = spread_weights(weights)

    ends = jnp.cumsum(doc_lengths)
    nblocks = GROUP * SIDE // BLOCK
    decays = lax.dynamic_slice(log_decay, (HH * z, 0), (HH, GROUP * SIDE))
    cum_all = jnp.cumsum(decays.reshape(HH, nblocks, BLOCK), axis=2)
    starts = jnp.arange(nblocks, dtype=jnp.int32) * BLOCK
    before_all = doc_of(starts - 1, ends)
    last_all = doc_of(starts + (BLOCK - 1), ends)
    pass_all = jnp.where((before_all == last_all)[None], jnp.exp(cum_all[:, :, -1]), 0.0)
    gpass = jnp.prod(pass_all.reshape(HH, SIDE, NB), axis=2)
    f1 = jnp.where(y >= 1, 1.0, 0.0) * jnp.ones((HH,), jnp.float32)
    prev1 = lax.dynamic_index_in_dim(gpass, jnp.maximum(y - 1, 0), 1, keepdims=False)
    prev2 = lax.dynamic_index_in_dim(gpass, jnp.maximum(y - 2, 0), 1, keepdims=False)
    f2 = jnp.where(y >= 2, prev1, 0.0)
    f3 = jnp.where(y >= 3, prev1 * prev2, 0.0)
    fac = jnp.stack([f1, f2, f3], axis=1)
    passes = lax.dynamic_slice_in_dim(pass_all, NB * y, NB, 1)
    carry = jnp.concatenate(
        [jnp.ones((HH, 1), jnp.float32), jnp.cumprod(passes, axis=1)[:, :-1]], axis=1
    )
    cum = lax.dynamic_slice_in_dim(cum_all, NB * y, NB, 1)
    before = lax.dynamic_slice_in_dim(before_all, NB * y, NB, 0)
    last = lax.dynamic_slice_in_dim(last_all, NB * y, NB, 0)
    points = GROUP * y + jnp.arange(GROUP, dtype=jnp.int32).reshape(NB, BLOCK)
    doc = doc_of(points, ends)
    qfac = jnp.where((doc == before[:, None])[None], jnp.exp(cum), 0.0)
    kfac = jnp.where((doc == last[:, None])[None], jnp.exp(cum[:, :, -1:] - cum), 0.0)
    cumc = cum.reshape(HH, GROUP).T
    qf = qfac.reshape(HH, GROUP).T
    kf = kfac.reshape(HH, GROUP).T
    docc = doc.reshape(GROUP, 1)

    own = call_project(place, tokens, w, [])
    proj = call_project(place, group, w, [own])

    smem = pl.BlockSpec(memory_space=pltpu.SMEM)
    vmem = pl.BlockSpec(memory_space=pltpu.VMEM)
    square = (HDIM, HDIM)
    local, final = pl.pallas_call(
        states,
        out_shape=(
            jax.ShapeDtypeStruct((HH, NB) + square, jnp.float32),
            jax.ShapeDtypeStruct((HH,) + square, jnp.bfloat16),
        ),
        in_specs=[vmem, vmem, smem],
        out_specs=(vmem, vmem),
        cost_estimate=pl.CostEstimate(flops=1 << 27, bytes_accessed=4 << 20, transcendentals=0),
        compiler_params=VMEM,
        name="states",
    )(proj, kf, passes)
    s1, s2, s3 = move_y(final, 1), move_y(final, 2), move_y(final, 3)
    intra = pl.pallas_call(
        intras,
        out_shape=jax.ShapeDtypeStruct((GROUP, HH * HDIM), jnp.float32),
        in_specs=[vmem] * 5,
        out_specs=vmem,
        cost_estimate=pl.CostEstimate(flops=1 << 30, bytes_accessed=8 << 20, transcendentals=1 << 20),
        compiler_params=VMEM,
        name="intras",
    )(proj, cum, cumc, doc, docc)
    att, squares = pl.pallas_call(
        inters,
        out_shape=(
            jax.ShapeDtypeStruct((GROUP, HH * HDIM), jnp.bfloat16),
            jax.ShapeDtypeStruct((NB, BLOCK), jnp.float32),
        ),
        in_specs=[vmem, vmem, smem, smem] + [vmem] * 5,
        out_specs=(vmem, vmem),
        cost_estimate=pl.CostEstimate(flops=1 << 28, bytes_accessed=8 << 20, transcendentals=0),
        compiler_params=VMEM,
        name="inters",
    )(proj, qf, carry, fac, local, s1, s2, s3, intra)

    near = SPAN // BLOCK

    def share(a, d, size):
        return lax.dynamic_slice_in_dim(a, ((z + d) % SIDE) * size, size, 0)

    part = share(squares, 0, near)
    for d in (1, -1, 2):
        part = part + move_z(share(squares, d, near), d)
    part = part + swap(part)
    total = part + move_x(part, 1) + move_x(part, -1) + move_x(part, 2)
    pieces = [share(att, 0, SPAN)] + [move_z(share(att, d, SPAN), d) for d in (1, -1, 2)]
    return pl.pallas_call(
        finish,
        out_shape=jax.ShapeDtypeStruct((SPAN, SIDE * HH * HDIM), jnp.bfloat16),
        in_specs=[smem] + [vmem] * 6,
        out_specs=vmem,
        cost_estimate=pl.CostEstimate(flops=1 << 22, bytes_accessed=3 << 20, transcendentals=0),
        compiler_params=VMEM,
        name="finish",
    )(place, total, norm_gain.reshape(1, -1), *pieces)


def solution(mesh):
    mesh = jax.sharding.Mesh(mesh.devices.reshape(SIDE, SIDE, SIDE, 2), AXES)
    in_specs = (
        P(("y", "z"), None),
        P(("y", "z"), None, ("x", "c")),
        P(("x", "c"), None),
        P(),
        P(("x", "c")),
    )
    out_specs = P(("y", "z"), ("x", "c"))
    return jax.shard_map(
        per_device, mesh=mesh, in_specs=in_specs, out_specs=out_specs, check_vma=False
    )
```

```python
import functools

import jax
import jax.numpy as jnp
from jax import lax
from jax.experimental import pallas as pl
from jax.experimental.pallas import tpu as pltpu
from jax.sharding import PartitionSpec as P

AXES = ("y", "z", "x", "c")
HEADS = 64
HDIM = 128
BLOCK = 256
SIDE = 4
SPAN = 512
DEPTH = 6144
WROWS = 384
HH = 2
COLS = 3 * HH * HDIM
GROUP = SIDE * SPAN
NB = GROUP // BLOCK
VMEM = pltpu.CompilerParams(vmem_limit_bytes=56 * 1024 * 1024)


def move_y(a, d):
    return lax.ppermute(a, "y", [(s, (s + d) % 4) for s in range(4)])


def move_z(a, d):
    return lax.ppermute(a, "z", [(s, (s + d) % 4) for s in range(4)])


def move_x(a, d):
    return lax.ppermute(a, "x", [(s, (s + d) % 4) for s in range(4)])


def swap(a):
    return lax.ppermute(a, "c", [(0, 1), (1, 0)])


def opposed(a, axis, d):
    perm = [(2 * s + c, 2 * ((s + d - 2 * d * c) % 4) + c) for s in range(4) for c in range(2)]
    return lax.ppermute(a, (axis, "c"), perm)


ORDER = (
    ("y00", ""),
    ("z1", ""),
    ("z3", ""),
    ("y01", ""),
    ("z2", "z1"),
    ("y02", "z2"),
    ("y10", "y01"),
    ("y30", "y02 z3"),
    ("y11", "y02"),
    ("y31", ""),
    ("y12", "y30"),
    ("y20", "y11"),
    ("y32", "y11"),
    ("y21", "y12"),
    ("y22", ""),
)


def spread_weights(weights):
    got = {"z0": weights[0]}
    for name, after in ORDER:
        if name[0] == "z":
            source = weights[int(name[1])]
        elif name[2] == "0":
            source = got["z" + name[1]]
        else:
            source = got["y" + name[1] + str(int(name[2]) - 1)]
        if after:
            source = lax.optimization_barrier((source, *[got[n] for n in after.split()]))[0]
        got[name] = opposed(source, name[0], int(name[1]) if name[0] == "z" else 1)
    return [
        got[n] for k in range(SIDE) for n in ["z%d" % k] + ["y%d%d" % (k, i) for i in range(3)]
    ]


def along(place, axis, steps):
    return lax.rem(place[axis] + SIDE + steps * (2 * place[3] - 1), SIDE)


def product(spans, place, x, wrefs, cols, wfull, acc, sem):
    step = pl.program_id(0)
    depth = SIDE * WROWS

    @pl.when(step == 0)
    def _():
        for i in range(SIDE):
            for k in range(SIDE):
                at = along(place, 1, i) * SIDE + along(place, 0, k)
                rows = pl.ds(pl.multiple_of(at * WROWS, WROWS), WROWS)
                pltpu.make_async_copy(
                    wrefs[SIDE * k + i].at[:, cols], wfull.at[rows], sem.at[at]
                ).start()
        for i in range(SIDE):
            for k in range(SIDE):
                rows = pl.ds((SIDE * i + k) * WROWS, WROWS)
                pltpu.make_async_copy(
                    wrefs[0].at[:, cols], wfull.at[rows], sem.at[SIDE * i + k]
                ).wait()
            part = jnp.dot(
                x[:, pl.ds(i * depth, depth)],
                wfull[pl.ds(i * depth, depth), :],
                preferred_element_type=jnp.float32,
            )
            if i == 0:
                acc[...] = part
            else:
                acc[...] += part

    if spans > 1:

        @pl.when(step > 0)
        def _():
            acc[...] = jnp.dot(x[...], wfull[...], preferred_element_type=jnp.float32)

    total = acc[...]
    return (total / (1.0 + jnp.exp(-total))).astype(jnp.bfloat16)


def span_of(spans, step, place):
    return place[0] if spans == 1 else lax.rem(place[0] + step + 1, SIDE)


def project_kv(spans, place, x, kf, suffix, before, *refs):
    wrefs = refs[: SIDE * SIDE]
    kv_out, block_out, sum_out, held, wfull, acc, sem = refs[-7:]
    step = pl.program_id(0)
    span = span_of(spans, step, place)
    kv_out[...] = product(
        spans, place, x, wrefs, pl.ds(HH * HDIM, 2 * HH * HDIM), wfull, acc, sem
    )

    @pl.when(step == 0)
    def _():
        held[...] = before[...]

    for b in range(SPAN // BLOCK):
        rows = pl.ds(b * BLOCK, BLOCK)
        for h in range(HH):
            k = kv_out[rows, pl.ds(h * HDIM, HDIM)].astype(jnp.float32)
            v = kv_out[rows, pl.ds((HH + h) * HDIM, HDIM)]
            kd = (k * kf[rows, pl.ds(h, 1)]).astype(jnp.bfloat16)
            kv = lax.dot_general(
                kd, v, (((0,), (0,)), ((), ())), preferred_element_type=jnp.float32
            )
            block_out[b, h] = kv
            held[h] += suffix[h, span * (SPAN // BLOCK) + b] * kv

    @pl.when(step == spans - 1)
    def _():
        sum_out[...] = held[...].astype(sum_out.dtype)


def project_q(spans, place, x, kv, decay, qf, *refs):
    wrefs = refs[: SIDE * SIDE]
    qd_out, intra_out, wfull, acc, sem = refs[-5:]
    q = product(spans, place, x, wrefs, pl.ds(0, HH * HDIM), wfull, acc, sem)
    for b in range(SPAN // BLOCK):
        rows = pl.ds(b * BLOCK, BLOCK)
        for h in range(HH):
            cols = pl.ds(h * HDIM, HDIM)
            qb = q[b * BLOCK : (b + 1) * BLOCK, h * HDIM : (h + 1) * HDIM]
            k = kv[rows, cols]
            v = kv[rows, pl.ds((HH + h) * HDIM, HDIM)]
            scores = lax.dot_general(
                qb, k, (((1,), (1,)), ((), ())), preferred_element_type=jnp.float32
            )
            weights = (scores * decay[b, h]).astype(jnp.bfloat16)
            intra_out[rows, cols] = jnp.dot(weights, v, preferred_element_type=jnp.float32)
            qd_out[rows, cols] = (qb.astype(jnp.float32) * qf[rows, pl.ds(h, 1)]).astype(
                jnp.bfloat16
            )


def call_project(place, rows, w, kf, qf, suffix, decay, before, held):
    spans = SIDE - 1 if held else 1
    near = SPAN // BLOCK
    square = (HDIM, HDIM)
    width = HH * HDIM
    hbm = pl.BlockSpec(memory_space=pl.ANY)
    smem = pl.BlockSpec(memory_space=pltpu.SMEM)

    def there(i, place):
        return (span_of(spans, i, place), 0)

    def blocks(i, place):
        return (span_of(spans, i, place), 0, 0, 0)

    def whole(i, place):
        return (0, 0, 0)

    xspec = pl.BlockSpec((SPAN, DEPTH), there if held else lambda i, place: (i, 0))
    column = pl.BlockSpec((SPAN, HH), there)
    nw = len(w)

    def scratch(cols):
        return [
            pltpu.VMEM((DEPTH, cols), jnp.bfloat16),
            pltpu.VMEM((SPAN, cols), jnp.float32),
            pltpu.SemaphoreType.DMA((SIDE * SIDE,)),
        ]

    def cost(cols):
        return pl.CostEstimate(
            flops=2 * spans * SPAN * DEPTH * cols,
            bytes_accessed=(6 + 8 * spans) << 20,
            transcendentals=0,
        )

    kv, states, total = pl.pallas_call(
        functools.partial(project_kv, spans),
        out_shape=(
            jax.ShapeDtypeStruct((GROUP, 2 * width), jnp.bfloat16),
            jax.ShapeDtypeStruct((NB, HH) + square, jnp.float32),
            jax.ShapeDtypeStruct((HH,) + square, jnp.bfloat16 if held else jnp.float32),
        ),
        grid_spec=pltpu.PrefetchScalarGridSpec(
            num_scalar_prefetch=1,
            grid=(spans,),
            in_specs=[xspec, column, smem, pl.BlockSpec((HH,) + square, whole)]
            + [hbm] * (nw + len(held[:2])),
            out_specs=(
                pl.BlockSpec((SPAN, 2 * width), there),
                pl.BlockSpec((near, HH) + square, blocks),
                pl.BlockSpec((HH,) + square, whole),
            ),
            scratch_shapes=[pltpu.VMEM((HH,) + square, jnp.float32)] + scratch(2 * width),
        ),
        input_output_aliases={5 + nw: 0, 6 + nw: 1} if held else {},
        cost_estimate=cost(2 * width),
        compiler_params=VMEM,
        name="kv_others" if held else "kv_own",
    )(place, rows, kf, suffix, before, *w, *held[:2])
    qd, intra = pl.pallas_call(
        functools.partial(project_q, spans),
        out_shape=(
            jax.ShapeDtypeStruct((GROUP, width), jnp.bfloat16),
            jax.ShapeDtypeStruct((GROUP, width), jnp.float32),
        ),
        grid_spec=pltpu.PrefetchScalarGridSpec(
            num_scalar_prefetch=1,
            grid=(spans,),
            in_specs=[
                xspec,
                pl.BlockSpec((SPAN, 2 * width), there),
                pl.BlockSpec((near, HH, BLOCK, BLOCK), blocks),
                column,
            ]
            + [hbm] * (nw + len(held[2:])),
            out_specs=(pl.BlockSpec((SPAN, width), there), pl.BlockSpec((SPAN, width), there)),
            scratch_shapes=scratch(width),
        ),
        input_output_aliases={5 + nw: 0, 6 + nw: 1} if held else {},
        cost_estimate=cost(width),
        compiler_params=VMEM,
        name="q_others" if held else "q_own",
    )(place, rows, kv, decay, qf, *w, *held[2:])
    return kv, states, total, qd, intra


def decays(cumr, cumc, docr, docc, out):
    row = lax.broadcasted_iota(jnp.int32, (BLOCK, BLOCK), 0)
    col = lax.broadcasted_iota(jnp.int32, (BLOCK, BLOCK), 1)
    mask = (row >= col) & (docc[...] == docr[0])
    for h in range(HH):
        diff = cumc[:, pl.ds(h, 1)] - cumr[0, pl.ds(h, 1), :]
        out[0, h] = jnp.where(mask, jnp.exp(jnp.where(mask, diff, 0.0)), 0.0)


def inters(place, qd, intra, states, passes, fac, s1, s2, s3, *refs):
    outs, squares_outs = refs[:SIDE], refs[SIDE : 2 * SIDE]
    state, att, squares, sem = refs[2 * SIDE :]
    b = pl.program_id(0)

    @pl.when(b == 0)
    def _():
        for h in range(HH):
            state[h] = (
                fac[h, 0] * s1[h].astype(jnp.float32)
                + fac[h, 1] * s2[h].astype(jnp.float32)
                + fac[h, 2] * s3[h].astype(jnp.float32)
            )

    near = SPAN // BLOCK
    span, part = b // near, lax.rem(b, near)
    rows = pl.ds(pl.multiple_of(part * BLOCK, BLOCK), BLOCK)
    sums = jnp.zeros((BLOCK, HDIM), jnp.float32)
    for h in range(HH):
        cols = pl.ds(h * HDIM, HDIM)
        value = intra[:, cols] + jnp.dot(
            qd[:, cols], state[h].astype(jnp.bfloat16), preferred_element_type=jnp.float32
        )
        sums += value * value
        att[span, rows, cols] = value.astype(jnp.bfloat16)
        state[h] = passes[h, b] * state[h] + states[0, h]
    ones = jnp.ones((8, HDIM), jnp.bfloat16)
    total = jnp.zeros((8, BLOCK), jnp.float32)
    for _ in range(3):
        piece = sums.astype(jnp.bfloat16)
        sums = sums - piece.astype(jnp.float32)
        total += lax.dot_general(
            ones, piece, (((1,), (1,)), ((), ())), preferred_element_type=jnp.float32
        )
    squares[span, part] = total

    @pl.when(b == NB - 1)
    def _():
        copies = []
        for i, d in enumerate((0, 1, 3, 2)):
            target = lax.rem(place[0] + d, SIDE)
            copies.append(pltpu.make_async_copy(att.at[target], outs[i], sem.at[2 * i]))
            copies.append(
                pltpu.make_async_copy(squares.at[target], squares_outs[i], sem.at[2 * i + 1])
            )
        for copy in copies:
            copy.start()
        for copy in copies:
            copy.wait()


def finish(place, total, gain, p0, p1, p2, p3, out):
    scale = lax.rsqrt(total[...] / (HEADS * HDIM) + 1e-05)
    for b in range(SPAN // BLOCK):
        rows = pl.ds(b * BLOCK, BLOCK)
        column = jnp.transpose(scale[b])[:, 0:1]
        for dz, piece in ((0, p0), (3, p1), (1, p2), (2, p3)):
            zz = lax.rem(place[0] + dz, SIDE)
            cols = pl.ds(pl.multiple_of(zz * (HH * HDIM), HH * HDIM), HH * HDIM)
            value = piece[rows, :].astype(jnp.float32) * column
            out[rows, cols] = (value * gain[0:1, cols]).astype(jnp.bfloat16)


def doc_of(points, ends):
    found = jnp.sum((points[..., None] >= ends).astype(jnp.int32), axis=-1)
    return jnp.where(points < 0, -1, found)


def per_device(tokens, w_qkv, log_decay, doc_lengths, norm_gain):
    y, z, x, c = [lax.axis_index(axis) for axis in AXES]
    place = jnp.stack([z, y, x, c]).astype(jnp.int32)

    mine = lax.dynamic_slice(tokens, ((2 * x + c) * 64, 0), (64, DEPTH))
    wview = w_qkv.reshape(WROWS, 3, SIDE, HH * HDIM)
    weights = []
    for d in range(SIDE):
        at = (z + d * (1 - 2 * c)) % SIDE
        weights.append(
            lax.dynamic_slice(wview, (0, 0, at, 0), (WROWS, 3, 1, HH * HDIM)).reshape(WROWS, COLS)
        )
    group = lax.all_gather(mine, ("z", "x", "c"), axis=0, tiled=True)
    w = spread_weights(weights)

    ends = jnp.cumsum(doc_lengths)
    nblocks = GROUP * SIDE // BLOCK
    logs = lax.dynamic_slice(log_decay, (HH * z, 0), (HH, GROUP * SIDE))
    cum_all = jnp.cumsum(logs.reshape(HH, nblocks, BLOCK), axis=2)
    starts = jnp.arange(nblocks, dtype=jnp.int32) * BLOCK
    before_all = doc_of(starts - 1, ends)
    last_all = doc_of(starts + (BLOCK - 1), ends)
    pass_all = jnp.where((before_all == last_all)[None], jnp.exp(cum_all[:, :, -1]), 0.0)
    gpass = jnp.prod(pass_all.reshape(HH, SIDE, NB), axis=2)
    f1 = jnp.where(y >= 1, 1.0, 0.0) * jnp.ones((HH,), jnp.float32)
    prev1 = lax.dynamic_index_in_dim(gpass, jnp.maximum(y - 1, 0), 1, keepdims=False)
    prev2 = lax.dynamic_index_in_dim(gpass, jnp.maximum(y - 2, 0), 1, keepdims=False)
    f2 = jnp.where(y >= 2, prev1, 0.0)
    f3 = jnp.where(y >= 3, prev1 * prev2, 0.0)
    fac = jnp.stack([f1, f2, f3], axis=1)
    passes = lax.dynamic_slice_in_dim(pass_all, NB * y, NB, 1)
    suffix = jnp.concatenate(
        [jnp.cumprod(passes[:, :0:-1], axis=1)[:, ::-1], jnp.ones((HH, 1), jnp.float32)], axis=1
    )
    cum = lax.dynamic_slice_in_dim(cum_all, NB * y, NB, 1)
    before = lax.dynamic_slice_in_dim(before_all, NB * y, NB, 0)
    last = lax.dynamic_slice_in_dim(last_all, NB * y, NB, 0)
    points = GROUP * y + jnp.arange(GROUP, dtype=jnp.int32).reshape(NB, BLOCK)
    doc = doc_of(points, ends)
    qfac = jnp.where((doc == before[:, None])[None], jnp.exp(cum), 0.0)
    kfac = jnp.where((doc == last[:, None])[None], jnp.exp(cum[:, :, -1:] - cum), 0.0)
    cumc = cum.reshape(HH, GROUP).T
    qf = qfac.reshape(HH, GROUP).T
    kf = kfac.reshape(HH, GROUP).T
    docc = doc.reshape(GROUP, 1)

    smem = pl.BlockSpec(memory_space=pltpu.SMEM)
    vmem = pl.BlockSpec(memory_space=pltpu.VMEM)
    hbm = pl.BlockSpec(memory_space=pl.ANY)
    square = (HDIM, HDIM)
    decay = pl.pallas_call(
        decays,
        out_shape=jax.ShapeDtypeStruct((NB, HH, BLOCK, BLOCK), jnp.float32),
        grid=(NB,),
        in_specs=[
            pl.BlockSpec((1, HH, BLOCK), lambda b: (b, 0, 0)),
            pl.BlockSpec((BLOCK, HH), lambda b: (b, 0)),
            pl.BlockSpec((1, 1, BLOCK), lambda b: (b, 0, 0)),
            pl.BlockSpec((BLOCK, 1), lambda b: (b, 0)),
        ],
        out_specs=pl.BlockSpec((1, HH, BLOCK, BLOCK), lambda b: (b, 0, 0, 0)),
        name="decays",
    )(jnp.transpose(cum, (1, 0, 2)), cumc, doc[:, None], docc)

    zero = jnp.zeros((HH,) + square, jnp.float32)
    kv, states, total, qd, intra = call_project(
        place, tokens, w, kf, qf, suffix, decay, zero, []
    )
    kv, states, total, qd, intra = call_project(
        place, group, w, kf, qf, suffix, decay, total, [kv, states, qd, intra]
    )
    s1, s2, s3 = move_y(total, 1), move_y(total, 2), move_y(total, 3)

    def block(b, place):
        return (b, 0)

    width = HH * HDIM
    near = SPAN // BLOCK
    summed = (near, 8, BLOCK)
    whole = pl.BlockSpec((HH,) + square, lambda b, place: (0, 0, 0))
    out = pl.pallas_call(
        inters,
        out_shape=[jax.ShapeDtypeStruct((SPAN, width), jnp.bfloat16)] * SIDE
        + [jax.ShapeDtypeStruct(summed, jnp.float32)] * SIDE,
        grid_spec=pltpu.PrefetchScalarGridSpec(
            num_scalar_prefetch=1,
            grid=(NB,),
            in_specs=[
                pl.BlockSpec((BLOCK, width), block),
                pl.BlockSpec((BLOCK, width), block),
                pl.BlockSpec((1, HH) + square, lambda b, place: (b, 0, 0, 0)),
                smem,
                smem,
                whole,
                whole,
                whole,
            ],
            out_specs=[hbm] * (2 * SIDE),
            scratch_shapes=[
                pltpu.VMEM((HH,) + square, jnp.float32),
                pltpu.VMEM((SIDE, SPAN, width), jnp.bfloat16),
                pltpu.VMEM((SIDE,) + summed, jnp.float32),
                pltpu.SemaphoreType.DMA((2 * SIDE,)),
            ],
        ),
        cost_estimate=pl.CostEstimate(flops=1 << 28, bytes_accessed=6 << 20, transcendentals=0),
        compiler_params=VMEM,
        name="inters",
    )(place, qd, intra, states, passes, fac, s1, s2, s3)

    part = out[SIDE]
    for i, d in enumerate((1, -1, 2)):
        part = part + move_z(out[SIDE + 1 + i], d)
    part = part + swap(part)
    part = part + move_x(part, 1) + move_x(part, -1) + move_x(part, 2)
    pieces = [out[0]] + [move_z(out[1 + i], d) for i, d in enumerate((1, -1, 2))]
    return pl.pallas_call(
        finish,
        out_shape=jax.ShapeDtypeStruct((SPAN, SIDE * width), jnp.bfloat16),
        in_specs=[smem] + [vmem] * 6,
        out_specs=vmem,
        cost_estimate=pl.CostEstimate(flops=1 << 22, bytes_accessed=3 << 20, transcendentals=0),
        compiler_params=VMEM,
        name="finish",
    )(place, part, norm_gain.reshape(1, -1), *pieces)


def solution(mesh):
    mesh = jax.sharding.Mesh(mesh.devices.reshape(SIDE, SIDE, SIDE, 2), AXES)
    in_specs = (
        P(("y", "z"), None),
        P(("y", "z"), None, ("x", "c")),
        P(("x", "c"), None),
        P(),
        P(("x", "c")),
    )
    out_specs = P(("y", "z"), ("x", "c"))
    return jax.shard_map(
        per_device, mesh=mesh, in_specs=in_specs, out_specs=out_specs, check_vma=False
    )
```

```python
import functools

import jax
import jax.numpy as jnp
from jax import lax
from jax.experimental import pallas as pl
from jax.experimental.pallas import tpu as pltpu
from jax.sharding import PartitionSpec as P

AXES = ("y", "z", "x", "c")
HEADS = 64
HDIM = 128
BLOCK = 256
SIDE = 4
SPAN = 512
DEPTH = 6144
WROWS = 384
HH = 2
COLS = 3 * HH * HDIM
GROUP = SIDE * SPAN
NB = GROUP // BLOCK
VMEM = pltpu.CompilerParams(vmem_limit_bytes=58 * 1024 * 1024)
SMALL = pltpu.CompilerParams(vmem_limit_bytes=24 * 1024 * 1024)


def move_y(a, d):
    return lax.ppermute(a, "y", [(s, (s + d) % 4) for s in range(4)])


def move_z(a, d):
    return lax.ppermute(a, "z", [(s, (s + d) % 4) for s in range(4)])


def move_x(a, d):
    return lax.ppermute(a, "x", [(s, (s + d) % 4) for s in range(4)])


def swap(a):
    return lax.ppermute(a, "c", [(0, 1), (1, 0)])


def opposed(a, axis, d):
    perm = [(2 * s + c, 2 * ((s + d - 2 * d * c) % 4) + c) for s in range(4) for c in range(2)]
    return lax.ppermute(a, (axis, "c"), perm)


ORDER = (
    ("y00", ""),
    ("z1", ""),
    ("z3", ""),
    ("z2", ""),
    ("y10", ""),
    ("y01", "z1"),
    ("y30", "y00"),
    ("y02", "z3"),
    ("y11", ""),
    ("y31", ""),
    ("y12", ""),
    ("y20", "y11 y02 early"),
    ("y32", ""),
    ("y21", ""),
    ("y22", ""),
)


def spread_weights(weights, early):
    got = {"z0": weights[0], "early": early}
    for name, after in ORDER:
        if name[0] == "z":
            source = weights[int(name[1])]
        elif name[2] == "0":
            source = got["z" + name[1]]
        else:
            source = got["y" + name[1] + str(int(name[2]) - 1)]
        if after:
            source = lax.optimization_barrier((source, *[got[n] for n in after.split()]))[0]
        got[name] = opposed(source, name[0], int(name[1]) if name[0] == "z" else 1)
    pieces = [
        got[n] for k in range(SIDE) for n in ["z%d" % k] + ["y%d%d" % (k, i) for i in range(3)]
    ]
    return pieces, (got["z1"], got["z3"])


def along(place, axis, steps):
    return lax.rem(place[axis] + SIDE + steps * (2 * place[3] - 1), SIDE)


def silu(total):
    return (total / (1.0 + jnp.exp(-total))).astype(jnp.bfloat16)


def project(others, place, x, *refs):
    wrefs = refs[: SIDE * SIDE]
    out, xbuf, wfull, acc, result, wsem, xsem, osem = refs[-8:]
    depth = SIDE * WROWS
    count = SIDE - 1 if others else 1
    spans = [lax.rem(place[0] + (j + 1 if others else 0), SIDE) for j in range(count)]
    tiles = [pl.ds(i * depth, depth) for i in range(SIDE)]

    def fetch_w(i):
        for k in range(SIDE):
            zz = along(place, 0, k)
            rows = pl.ds(pl.multiple_of(i * depth + zz * WROWS, WROWS), WROWS)
            n = SIDE * k + i
            yield pltpu.make_async_copy(wrefs[n], wfull.at[rows], wsem.at[n])

    def fetch_x(j, i):
        source = x.at[spans[j]] if others else x
        cols = pl.ds(pl.multiple_of(along(place, 1, i) * depth, depth), depth)
        return pltpu.make_async_copy(
            source.at[:, cols], xbuf.at[j, :, tiles[i]], xsem.at[SIDE * j + i]
        )

    def start(i):
        for copy in fetch_w(i):
            copy.start()
        fetch_x(0, i).start()

    start(0)
    for i in range(SIDE):
        if i + 1 < SIDE:
            start(i + 1)
        else:
            for j in range(1, count):
                for t in range(SIDE):
                    fetch_x(j, t).start()
        for copy in fetch_w(i):
            copy.wait()
        fetch_x(0, i).wait()
        part = jnp.dot(
            xbuf[0, :, tiles[i]], wfull[tiles[i], :], preferred_element_type=jnp.float32
        )
        if i == 0:
            acc[...] = part
        elif i + 1 < SIDE:
            acc[...] += part
        else:
            result[0] = silu(acc[...] + part)
    pltpu.make_async_copy(result.at[0], out.at[spans[0]], osem.at[0]).start()
    for j in range(1, count):
        for i in range(SIDE):
            fetch_x(j, i).wait()
        for m in range(0, SPAN, BLOCK):
            rows = pl.ds(m, BLOCK)
            result[j, rows, :] = silu(
                jnp.dot(xbuf[j, rows, :], wfull[...], preferred_element_type=jnp.float32)
            )
        pltpu.make_async_copy(result.at[j], out.at[spans[j]], osem.at[j]).start()
    for j in range(count):
        pltpu.make_async_copy(result.at[j], out.at[spans[j]], osem.at[j]).wait()


def call_project(place, x, w, held):
    count = SIDE - 1 if held else 1
    smem = pl.BlockSpec(memory_space=pltpu.SMEM)
    hbm = pl.BlockSpec(memory_space=pl.ANY)
    return pl.pallas_call(
        functools.partial(project, bool(held)),
        out_shape=jax.ShapeDtypeStruct((SIDE, SPAN, COLS), jnp.bfloat16),
        in_specs=[smem] + [hbm] * (1 + len(w) + len(held)),
        out_specs=hbm,
        scratch_shapes=[
            pltpu.VMEM((count, SPAN, DEPTH), jnp.bfloat16),
            pltpu.VMEM((DEPTH, COLS), jnp.bfloat16),
            pltpu.VMEM((SPAN, COLS), jnp.float32),
            pltpu.VMEM((count, SPAN, COLS), jnp.bfloat16),
            pltpu.SemaphoreType.DMA((SIDE * SIDE,)),
            pltpu.SemaphoreType.DMA((SIDE * count,)),
            pltpu.SemaphoreType.DMA((count,)),
        ],
        input_output_aliases={2 + len(w): 0} if held else {},
        cost_estimate=pl.CostEstimate(
            flops=2 * count * SPAN * DEPTH * COLS,
            bytes_accessed=(10 + 7 * count) << 20,
            transcendentals=0,
        ),
        compiler_params=VMEM,
        name="project_others" if held else "project_own",
    )(place, x, *w, *held)


def decays(cumr, cumc, docr, docc, out):
    row = lax.broadcasted_iota(jnp.int32, (BLOCK, BLOCK), 0)
    col = lax.broadcasted_iota(jnp.int32, (BLOCK, BLOCK), 1)
    mask = (row >= col) & (docc[...] == docr[0])
    for h in range(HH):
        diff = cumc[:, pl.ds(h, 1)] - cumr[0, pl.ds(h, 1), :]
        out[0, h] = jnp.where(mask, jnp.exp(jnp.where(mask, diff, 0.0)), 0.0)


def block_states(keys, values, kf, suffix, states, total):
    for h in range(HH):
        held = jnp.zeros((HDIM, HDIM), jnp.float32)
        for b in range(NB):
            rows = pl.ds(b * BLOCK, BLOCK)
            k = keys[rows, pl.ds(h * HDIM, HDIM)].astype(jnp.float32)
            v = values[rows, pl.ds(h * HDIM, HDIM)]
            kd = (k * kf[rows, pl.ds(h, 1)]).astype(jnp.bfloat16)
            state = lax.dot_general(
                kd, v, (((0,), (0,)), ((), ())), preferred_element_type=jnp.float32
            )
            states[b, h] = state
            held += suffix[h, b] * state
        total[h] = held.astype(jnp.bfloat16)


def intras(proj, decay, qf, qd_out, out):
    for h in range(HH):
        cols = pl.ds(h * HDIM, HDIM)
        q = proj[:, cols]
        k = proj[:, pl.ds((HH + h) * HDIM, HDIM)]
        v = proj[:, pl.ds((2 * HH + h) * HDIM, HDIM)]
        scores = lax.dot_general(
            q, k, (((1,), (1,)), ((), ())), preferred_element_type=jnp.float32
        )
        weights = (scores * decay[0, h]).astype(jnp.bfloat16)
        out[:, cols] = jnp.dot(weights, v, preferred_element_type=jnp.float32)
        qd_out[:, cols] = (q.astype(jnp.float32) * qf[:, pl.ds(h, 1)]).astype(jnp.bfloat16)


def inters(place, qd, intra, states, passes, fac, s1, s2, s3, *refs):
    outs, squares_outs = refs[:SIDE], refs[SIDE : 2 * SIDE]
    att, squares, sem = refs[2 * SIDE :]
    near = SPAN // BLOCK
    ones = jnp.ones((8, HDIM), jnp.bfloat16)
    state = [
        fac[h, 0] * s1[h].astype(jnp.float32)
        + fac[h, 1] * s2[h].astype(jnp.float32)
        + fac[h, 2] * s3[h].astype(jnp.float32)
        for h in range(HH)
    ]
    for b in range(NB):
        rows = pl.ds(b * BLOCK, BLOCK)
        sums = jnp.zeros((BLOCK, HDIM), jnp.float32)
        for h in range(HH):
            cols = pl.ds(h * HDIM, HDIM)
            value = intra[rows, cols] + jnp.dot(
                qd[rows, cols], state[h].astype(jnp.bfloat16), preferred_element_type=jnp.float32
            )
            sums += value * value
            att[b // near, pl.ds((b % near) * BLOCK, BLOCK), cols] = value.astype(jnp.bfloat16)
            state[h] = passes[h, b] * state[h] + states[b, h]
        total = jnp.zeros((8, BLOCK), jnp.float32)
        for _ in range(3):
            piece = sums.astype(jnp.bfloat16)
            sums = sums - piece.astype(jnp.float32)
            total += lax.dot_general(
                ones, piece, (((1,), (1,)), ((), ())), preferred_element_type=jnp.float32
            )
        squares[b // near, b % near] = total
    copies = []
    for i, d in enumerate((0, 1, 3, 2)):
        target = lax.rem(place[0] + d, SIDE)
        copies.append(pltpu.make_async_copy(squares.at[target], squares_outs[i], sem.at[2 * i]))
        copies.append(pltpu.make_async_copy(att.at[target], outs[i], sem.at[2 * i + 1]))
    for copy in copies:
        copy.start()
    for copy in copies:
        copy.wait()


def finish(place, total, gain, p0, p1, p2, p3, out):
    scale = lax.rsqrt(total[...] / (HEADS * HDIM) + 1e-05)
    for b in range(SPAN // BLOCK):
        rows = pl.ds(b * BLOCK, BLOCK)
        column = jnp.transpose(scale[b])[:, 0:1]
        for dz, piece in ((0, p0), (3, p1), (1, p2), (2, p3)):
            zz = lax.rem(place[0] + dz, SIDE)
            cols = pl.ds(pl.multiple_of(zz * (HH * HDIM), HH * HDIM), HH * HDIM)
            value = piece[rows, :].astype(jnp.float32) * column
            out[rows, cols] = (value * gain[0:1, cols]).astype(jnp.bfloat16)


def doc_of(points, ends):
    found = jnp.sum((points[..., None] >= ends).astype(jnp.int32), axis=-1)
    return jnp.where(points < 0, -1, found)


def per_device(tokens, w_qkv, log_decay, doc_lengths, norm_gain):
    y, z, x, c = [lax.axis_index(axis) for axis in AXES]
    place = jnp.stack([z, y, x, c]).astype(jnp.int32)

    ends = jnp.cumsum(doc_lengths)
    nblocks = GROUP * SIDE // BLOCK
    logs = lax.dynamic_slice(log_decay, (HH * z, 0), (HH, GROUP * SIDE))
    cum_all = jnp.cumsum(logs.reshape(HH, nblocks, BLOCK), axis=2)
    starts = jnp.arange(nblocks, dtype=jnp.int32) * BLOCK
    before_all = doc_of(starts - 1, ends)
    last_all = doc_of(starts + (BLOCK - 1), ends)
    pass_all = jnp.where((before_all == last_all)[None], jnp.exp(cum_all[:, :, -1]), 0.0)
    gpass = jnp.prod(pass_all.reshape(HH, SIDE, NB), axis=2)
    f1 = jnp.where(y >= 1, 1.0, 0.0) * jnp.ones((HH,), jnp.float32)
    prev1 = lax.dynamic_index_in_dim(gpass, jnp.maximum(y - 1, 0), 1, keepdims=False)
    prev2 = lax.dynamic_index_in_dim(gpass, jnp.maximum(y - 2, 0), 1, keepdims=False)
    f2 = jnp.where(y >= 2, prev1, 0.0)
    f3 = jnp.where(y >= 3, prev1 * prev2, 0.0)
    fac = jnp.stack([f1, f2, f3], axis=1)
    passes = lax.dynamic_slice_in_dim(pass_all, NB * y, NB, 1)
    suffix = jnp.concatenate(
        [jnp.cumprod(passes[:, :0:-1], axis=1)[:, ::-1], jnp.ones((HH, 1), jnp.float32)], axis=1
    )
    cum = lax.dynamic_slice_in_dim(cum_all, NB * y, NB, 1)
    before = lax.dynamic_slice_in_dim(before_all, NB * y, NB, 0)
    last = lax.dynamic_slice_in_dim(last_all, NB * y, NB, 0)
    points = GROUP * y + jnp.arange(GROUP, dtype=jnp.int32).reshape(NB, BLOCK)
    doc = doc_of(points, ends)
    qfac = jnp.where((doc == before[:, None])[None], jnp.exp(cum), 0.0)
    kfac = jnp.where((doc == last[:, None])[None], jnp.exp(cum[:, :, -1:] - cum), 0.0)
    cumc = cum.reshape(HH, GROUP).T
    qf = qfac.reshape(HH, GROUP).T
    kf = kfac.reshape(HH, GROUP).T
    docc = doc.reshape(GROUP, 1)

    smem = pl.BlockSpec(memory_space=pltpu.SMEM)
    vmem = pl.BlockSpec(memory_space=pltpu.VMEM)
    hbm = pl.BlockSpec(memory_space=pl.ANY)
    square = (HDIM, HDIM)
    width = HH * HDIM
    near = SPAN // BLOCK
    summed = (near, 8, BLOCK)
    decay = pl.pallas_call(
        decays,
        out_shape=jax.ShapeDtypeStruct((NB, HH, BLOCK, BLOCK), jnp.float32),
        grid=(NB,),
        in_specs=[
            pl.BlockSpec((1, HH, BLOCK), lambda b: (b, 0, 0)),
            pl.BlockSpec((BLOCK, HH), lambda b: (b, 0)),
            pl.BlockSpec((1, 1, BLOCK), lambda b: (b, 0, 0)),
            pl.BlockSpec((BLOCK, 1), lambda b: (b, 0)),
        ],
        out_specs=pl.BlockSpec((1, HH, BLOCK, BLOCK), lambda b: (b, 0, 0, 0)),
        compiler_params=SMALL,
        name="decays",
    )(jnp.transpose(cum, (1, 0, 2)), cumc, doc[:, None], docc)

    wview = w_qkv.reshape(WROWS, 3, SIDE, width)
    weights = []
    for d in range(SIDE):
        at = (z + d * (1 - 2 * c)) % SIDE
        weights.append(
            lax.dynamic_slice(wview, (0, 0, at, 0), (WROWS, 3, 1, width)).reshape(WROWS, COLS)
        )
    w, first = spread_weights(weights, (decay, kf, qf, suffix, passes, fac))
    mine = lax.dynamic_slice(tokens, ((2 * x + c) * 64, 0), (64, DEPTH))
    mine = lax.optimization_barrier((mine, *first))[0]
    group = lax.all_gather(mine, ("z", "x", "c"), axis=0, tiled=True)

    proj = call_project(place, tokens, w, [])
    proj = call_project(place, group.reshape(SIDE, SPAN, DEPTH), w, [proj])
    proj = proj.reshape(GROUP, COLS)
    states, total = pl.pallas_call(
        block_states,
        out_shape=(
            jax.ShapeDtypeStruct((NB, HH) + square, jnp.float32),
            jax.ShapeDtypeStruct((HH,) + square, jnp.bfloat16),
        ),
        grid=(1,),
        in_specs=[
            pl.BlockSpec((GROUP, width), lambda i: (0, 1)),
            pl.BlockSpec((GROUP, width), lambda i: (0, 2)),
            vmem,
            smem,
        ],
        out_specs=(vmem, vmem),
        cost_estimate=pl.CostEstimate(flops=1 << 27, bytes_accessed=4 << 20, transcendentals=0),
        compiler_params=SMALL,
        name="states",
    )(proj, proj, kf, suffix)
    s1, s2, s3 = move_y(total, 1), move_y(total, 2), move_y(total, 3)

    def block(b):
        return (b, 0)

    qd, intra = pl.pallas_call(
        intras,
        out_shape=(
            jax.ShapeDtypeStruct((GROUP, width), jnp.bfloat16),
            jax.ShapeDtypeStruct((GROUP, width), jnp.float32),
        ),
        grid=(NB,),
        in_specs=[
            pl.BlockSpec((BLOCK, COLS), block),
            pl.BlockSpec((1, HH, BLOCK, BLOCK), lambda b: (b, 0, 0, 0)),
            pl.BlockSpec((BLOCK, HH), block),
        ],
        out_specs=(pl.BlockSpec((BLOCK, width), block), pl.BlockSpec((BLOCK, width), block)),
        cost_estimate=pl.CostEstimate(flops=1 << 30, bytes_accessed=8 << 20, transcendentals=0),
        compiler_params=SMALL,
        name="intras",
    )(proj, decay, qf)
    out = pl.pallas_call(
        inters,
        out_shape=[jax.ShapeDtypeStruct((SPAN, width), jnp.bfloat16)] * SIDE
        + [jax.ShapeDtypeStruct(summed, jnp.float32)] * SIDE,
        in_specs=[smem, vmem, vmem, vmem, smem, smem, vmem, vmem, vmem],
        out_specs=[hbm] * (2 * SIDE),
        scratch_shapes=[
            pltpu.VMEM((SIDE, SPAN, width), jnp.bfloat16),
            pltpu.VMEM((SIDE,) + summed, jnp.float32),
            pltpu.SemaphoreType.DMA((2 * SIDE,)),
        ],
        cost_estimate=pl.CostEstimate(flops=1 << 28, bytes_accessed=6 << 20, transcendentals=0),
        compiler_params=SMALL,
        name="inters",
    )(place, qd, intra, states, passes, fac, s1, s2, s3)

    part = out[SIDE]
    for i, d in enumerate((1, -1, 2)):
        part = part + move_z(out[SIDE + 1 + i], d)
    part = part + swap(part)
    part = part + move_x(part, 1) + move_x(part, -1) + move_x(part, 2)
    pieces = [out[0]] + [move_z(out[1 + i], d) for i, d in enumerate((1, -1, 2))]
    return pl.pallas_call(
        finish,
        out_shape=jax.ShapeDtypeStruct((SPAN, SIDE * width), jnp.bfloat16),
        in_specs=[smem] + [vmem] * 6,
        out_specs=vmem,
        cost_estimate=pl.CostEstimate(flops=1 << 22, bytes_accessed=3 << 20, transcendentals=0),
        compiler_params=SMALL,
        name="finish",
    )(place, part, norm_gain.reshape(1, -1), *pieces)


def solution(mesh):
    mesh = jax.sharding.Mesh(mesh.devices.reshape(SIDE, SIDE, SIDE, 2), AXES)
    in_specs = (
        P(("y", "z"), None),
        P(("y", "z"), None, ("x", "c")),
        P(("x", "c"), None),
        P(),
        P(("x", "c")),
    )
    out_specs = P(("y", "z"), ("x", "c"))
    return jax.shard_map(
        per_device, mesh=mesh, in_specs=in_specs, out_specs=out_specs, check_vma=False
    )
```

```python
import functools

import jax
import jax.numpy as jnp
from jax import lax
from jax.experimental import pallas as pl
from jax.experimental.pallas import tpu as pltpu
from jax.sharding import PartitionSpec as P

AXES = ("y", "z", "x", "c")
HEADS = 64
HDIM = 128
BLOCK = 256
SIDE = 4
SPAN = 512
DEPTH = 6144
WROWS = 384
HH = 2
COLS = 3 * HH * HDIM
GROUP = SIDE * SPAN
NB = GROUP // BLOCK
VMEM = pltpu.CompilerParams(vmem_limit_bytes=58 * 1024 * 1024)
SMALL = pltpu.CompilerParams(vmem_limit_bytes=24 * 1024 * 1024)


def move_y(a, d):
    return lax.ppermute(a, "y", [(s, (s + d) % 4) for s in range(4)])


def move_z(a, d):
    return lax.ppermute(a, "z", [(s, (s + d) % 4) for s in range(4)])


def move_x(a, d):
    return lax.ppermute(a, "x", [(s, (s + d) % 4) for s in range(4)])


def swap(a):
    return lax.ppermute(a, "c", [(0, 1), (1, 0)])


def opposed(a, axis, d):
    perm = [(2 * s + c, 2 * ((s + d - 2 * d * c) % 4) + c) for s in range(4) for c in range(2)]
    return lax.ppermute(a, (axis, "c"), perm)


ORDER = (
    ("y00", ""),
    ("z1", ""),
    ("z3", ""),
    ("z2", ""),
    ("y10", ""),
    ("y01", "z1"),
    ("y30", "y00"),
    ("y02", "z3"),
    ("y11", ""),
    ("y31", ""),
    ("y12", ""),
    ("y20", "y11 y02 early"),
    ("y32", ""),
    ("y21", ""),
    ("y22", ""),
)


def spread_weights(weights, early):
    got = {"z0": weights[0], "early": early}
    for name, after in ORDER:
        if name[0] == "z":
            source = weights[int(name[1])]
        elif name[2] == "0":
            source = got["z" + name[1]]
        else:
            source = got["y" + name[1] + str(int(name[2]) - 1)]
        if after:
            source = lax.optimization_barrier((source, *[got[n] for n in after.split()]))[0]
        got[name] = opposed(source, name[0], int(name[1]) if name[0] == "z" else 1)
    pieces = [
        got[n] for k in range(SIDE) for n in ["z%d" % k] + ["y%d%d" % (k, i) for i in range(3)]
    ]
    return pieces, (got["z1"], got["z3"])


def along(place, axis, steps):
    return lax.rem(place[axis] + SIDE + steps * (2 * place[3] - 1), SIDE)


def silu(total):
    half = 0.5 * total
    return (half + half * jnp.tanh(half)).astype(jnp.bfloat16)


def project_own(place, x, *refs):
    wrefs = refs[: SIDE * SIDE]
    out, wout, xbuf, wfull, result, wsem, xsem, osem = refs[-8:]
    copies = [pltpu.make_async_copy(x, xbuf, xsem.at[0])]
    for k in range(SIDE):
        for i in range(SIDE):
            at = along(place, 1, i) * SIDE + along(place, 0, k)
            rows = pl.ds(pl.multiple_of(at * WROWS, WROWS), WROWS)
            n = SIDE * k + i
            copies.append(pltpu.make_async_copy(wrefs[n], wfull.at[rows], wsem.at[n]))
    for copy in copies:
        copy.start()
    for copy in copies:
        copy.wait()
    outs = [pltpu.make_async_copy(wfull, wout, osem.at[0])]
    outs[0].start()
    for m in range(0, SPAN, BLOCK):
        rows = pl.ds(m, BLOCK)
        result[rows, :] = silu(
            jnp.dot(xbuf[rows, :], wfull[...], preferred_element_type=jnp.float32)
        )
    outs.append(pltpu.make_async_copy(result, out.at[place[0]], osem.at[1]))
    outs[1].start()
    for copy in outs:
        copy.wait()


def project_others(place, x, w, own, out, wfull, sem):
    depth = DEPTH // SIDE
    step = pl.program_id(0)

    @pl.when(step == 0)
    def _():
        tiles = [pl.ds(i * depth, depth) for i in range(SIDE)]
        copies = [
            pltpu.make_async_copy(w.at[t], wfull.at[t], sem.at[i]) for i, t in enumerate(tiles)
        ]
        for copy in copies:
            copy.start()
        total = None
        for copy, t in zip(copies, tiles):
            copy.wait()
            part = jnp.dot(x[0, :, t], wfull[t, :], preferred_element_type=jnp.float32)
            total = part if total is None else total + part
        out[0] = silu(total)

    @pl.when(step > 0)
    def _():
        out[0] = silu(jnp.dot(x[0], wfull[...], preferred_element_type=jnp.float32))


def call_project(place, tokens, group, w):
    smem = pl.BlockSpec(memory_space=pltpu.SMEM)
    hbm = pl.BlockSpec(memory_space=pl.ANY)
    shape = jax.ShapeDtypeStruct((SIDE, SPAN, COLS), jnp.bfloat16)
    whole = (DEPTH, COLS)

    def cost(count):
        return pl.CostEstimate(
            flops=2 * count * SPAN * DEPTH * COLS,
            bytes_accessed=(10 + 7 * count) << 20,
            transcendentals=0,
        )

    own, wfull = pl.pallas_call(
        project_own,
        out_shape=(shape, jax.ShapeDtypeStruct(whole, jnp.bfloat16)),
        in_specs=[smem] + [hbm] * (1 + len(w)),
        out_specs=(hbm, hbm),
        scratch_shapes=[
            pltpu.VMEM((SPAN, DEPTH), jnp.bfloat16),
            pltpu.VMEM(whole, jnp.bfloat16),
            pltpu.VMEM((SPAN, COLS), jnp.bfloat16),
            pltpu.SemaphoreType.DMA((SIDE * SIDE,)),
            pltpu.SemaphoreType.DMA((1,)),
            pltpu.SemaphoreType.DMA((2,)),
        ],
        cost_estimate=cost(1),
        compiler_params=VMEM,
        name="project_own",
    )(place, tokens, *w)
    count = SIDE - 1
    parts = SPAN // BLOCK

    def there(i, place):
        return (lax.rem(place[0] + i // parts + 1, SIDE), i % parts, 0)

    return pl.pallas_call(
        project_others,
        out_shape=shape,
        grid_spec=pltpu.PrefetchScalarGridSpec(
            num_scalar_prefetch=1,
            grid=(count * parts,),
            in_specs=[
                pl.BlockSpec((1, BLOCK, DEPTH), there),
                hbm,
                hbm,
            ],
            out_specs=pl.BlockSpec((1, BLOCK, COLS), there),
            scratch_shapes=[
                pltpu.VMEM(whole, jnp.bfloat16),
                pltpu.SemaphoreType.DMA((SIDE,)),
            ],
        ),
        input_output_aliases={3: 0},
        cost_estimate=cost(count),
        compiler_params=VMEM,
        name="project_others",
    )(place, group, wfull, own)


def decays(cumr, cumc, docr, docc, out):
    row = lax.broadcasted_iota(jnp.int32, (BLOCK, BLOCK), 0)
    col = lax.broadcasted_iota(jnp.int32, (BLOCK, BLOCK), 1)
    mask = (row >= col) & (docc[...] == docr[0])
    for h in range(HH):
        diff = cumc[:, pl.ds(h, 1)] - cumr[0, pl.ds(h, 1), :]
        out[0, h] = jnp.where(mask, jnp.exp(jnp.where(mask, diff, 0.0)), 0.0)


def block_states(keys, values, kf, suffix, states, total):
    for h in range(HH):
        held = jnp.zeros((HDIM, HDIM), jnp.float32)
        for b in range(NB):
            rows = pl.ds(b * BLOCK, BLOCK)
            k = keys[rows, pl.ds(h * HDIM, HDIM)].astype(jnp.float32)
            v = values[rows, pl.ds(h * HDIM, HDIM)]
            kd = (k * kf[rows, pl.ds(h, 1)]).astype(jnp.bfloat16)
            state = lax.dot_general(
                kd, v, (((0,), (0,)), ((), ())), preferred_element_type=jnp.float32
            )
            states[b, h] = state
            held += suffix[h, b] * state
        total[h] = held.astype(jnp.bfloat16)


def intras(proj, decay, qf, qd_out, out):
    for h in range(HH):
        cols = pl.ds(h * HDIM, HDIM)
        q = proj[:, cols]
        k = proj[:, pl.ds((HH + h) * HDIM, HDIM)]
        v = proj[:, pl.ds((2 * HH + h) * HDIM, HDIM)]
        scores = lax.dot_general(
            q, k, (((1,), (1,)), ((), ())), preferred_element_type=jnp.float32
        )
        weights = (scores * decay[0, h]).astype(jnp.bfloat16)
        out[:, cols] = jnp.dot(weights, v, preferred_element_type=jnp.float32)
        qd_out[:, cols] = (q.astype(jnp.float32) * qf[:, pl.ds(h, 1)]).astype(jnp.bfloat16)


def inters(place, qd, intra, states, passes, fac, s1, s2, s3, *refs):
    outs, squares_outs = refs[:SIDE], refs[SIDE : 2 * SIDE]
    att, squares, sem = refs[2 * SIDE :]
    near = SPAN // BLOCK
    ones = jnp.ones((8, HDIM), jnp.bfloat16)
    state = [
        fac[h, 0] * s1[h].astype(jnp.float32)
        + fac[h, 1] * s2[h].astype(jnp.float32)
        + fac[h, 2] * s3[h].astype(jnp.float32)
        for h in range(HH)
    ]
    for b in range(NB):
        rows = pl.ds(b * BLOCK, BLOCK)
        sums = jnp.zeros((BLOCK, HDIM), jnp.float32)
        for h in range(HH):
            cols = pl.ds(h * HDIM, HDIM)
            value = intra[rows, cols] + jnp.dot(
                qd[rows, cols], state[h].astype(jnp.bfloat16), preferred_element_type=jnp.float32
            )
            sums += value * value
            att[b // near, pl.ds((b % near) * BLOCK, BLOCK), cols] = value.astype(jnp.bfloat16)
            state[h] = passes[h, b] * state[h] + states[b, h]
        total = jnp.zeros((8, BLOCK), jnp.float32)
        for _ in range(3):
            piece = sums.astype(jnp.bfloat16)
            sums = sums - piece.astype(jnp.float32)
            total += lax.dot_general(
                ones, piece, (((1,), (1,)), ((), ())), preferred_element_type=jnp.float32
            )
        squares[b // near, b % near] = total
    copies = []
    for i, d in enumerate((0, 1, 3, 2)):
        target = lax.rem(place[0] + d, SIDE)
        copies.append(pltpu.make_async_copy(squares.at[target], squares_outs[i], sem.at[2 * i]))
        copies.append(pltpu.make_async_copy(att.at[target], outs[i], sem.at[2 * i + 1]))
    for copy in copies:
        copy.start()
    for copy in copies:
        copy.wait()


def finish(place, total, gain, p0, p1, p2, p3, out):
    scale = lax.rsqrt(total[...] / (HEADS * HDIM) + 1e-05)
    for b in range(SPAN // BLOCK):
        rows = pl.ds(b * BLOCK, BLOCK)
        column = jnp.transpose(scale[b])[:, 0:1]
        for dz, piece in ((0, p0), (3, p1), (1, p2), (2, p3)):
            zz = lax.rem(place[0] + dz, SIDE)
            cols = pl.ds(pl.multiple_of(zz * (HH * HDIM), HH * HDIM), HH * HDIM)
            value = piece[rows, :].astype(jnp.float32) * column
            out[rows, cols] = (value * gain[0:1, cols]).astype(jnp.bfloat16)


def doc_of(points, ends):
    found = jnp.sum((points[..., None] >= ends).astype(jnp.int32), axis=-1)
    return jnp.where(points < 0, -1, found)


def per_device(tokens, w_qkv, log_decay, doc_lengths, norm_gain):
    y, z, x, c = [lax.axis_index(axis) for axis in AXES]
    place = jnp.stack([z, y, x, c]).astype(jnp.int32)

    ends = jnp.cumsum(doc_lengths)
    nblocks = GROUP * SIDE // BLOCK
    logs = lax.dynamic_slice(log_decay, (HH * z, 0), (HH, GROUP * SIDE))
    cum_all = jnp.cumsum(logs.reshape(HH, nblocks, BLOCK), axis=2)
    starts = jnp.arange(nblocks, dtype=jnp.int32) * BLOCK
    before_all = doc_of(starts - 1, ends)
    last_all = doc_of(starts + (BLOCK - 1), ends)
    pass_all = jnp.where((before_all == last_all)[None], jnp.exp(cum_all[:, :, -1]), 0.0)
    gpass = jnp.prod(pass_all.reshape(HH, SIDE, NB), axis=2)
    f1 = jnp.where(y >= 1, 1.0, 0.0) * jnp.ones((HH,), jnp.float32)
    prev1 = lax.dynamic_index_in_dim(gpass, jnp.maximum(y - 1, 0), 1, keepdims=False)
    prev2 = lax.dynamic_index_in_dim(gpass, jnp.maximum(y - 2, 0), 1, keepdims=False)
    f2 = jnp.where(y >= 2, prev1, 0.0)
    f3 = jnp.where(y >= 3, prev1 * prev2, 0.0)
    fac = jnp.stack([f1, f2, f3], axis=1)
    passes = lax.dynamic_slice_in_dim(pass_all, NB * y, NB, 1)
    suffix = jnp.concatenate(
        [jnp.cumprod(passes[:, :0:-1], axis=1)[:, ::-1], jnp.ones((HH, 1), jnp.float32)], axis=1
    )
    cum = lax.dynamic_slice_in_dim(cum_all, NB * y, NB, 1)
    before = lax.dynamic_slice_in_dim(before_all, NB * y, NB, 0)
    last = lax.dynamic_slice_in_dim(last_all, NB * y, NB, 0)
    points = GROUP * y + jnp.arange(GROUP, dtype=jnp.int32).reshape(NB, BLOCK)
    doc = doc_of(points, ends)
    qfac = jnp.where((doc == before[:, None])[None], jnp.exp(cum), 0.0)
    kfac = jnp.where((doc == last[:, None])[None], jnp.exp(cum[:, :, -1:] - cum), 0.0)
    cumc = cum.reshape(HH, GROUP).T
    qf = qfac.reshape(HH, GROUP).T
    kf = kfac.reshape(HH, GROUP).T
    docc = doc.reshape(GROUP, 1)

    smem = pl.BlockSpec(memory_space=pltpu.SMEM)
    vmem = pl.BlockSpec(memory_space=pltpu.VMEM)
    hbm = pl.BlockSpec(memory_space=pl.ANY)
    square = (HDIM, HDIM)
    width = HH * HDIM
    near = SPAN // BLOCK
    summed = (near, 8, BLOCK)
    decay = pl.pallas_call(
        decays,
        out_shape=jax.ShapeDtypeStruct((NB, HH, BLOCK, BLOCK), jnp.float32),
        grid=(NB,),
        in_specs=[
            pl.BlockSpec((1, HH, BLOCK), lambda b: (b, 0, 0)),
            pl.BlockSpec((BLOCK, HH), lambda b: (b, 0)),
            pl.BlockSpec((1, 1, BLOCK), lambda b: (b, 0, 0)),
            pl.BlockSpec((BLOCK, 1), lambda b: (b, 0)),
        ],
        out_specs=pl.BlockSpec((1, HH, BLOCK, BLOCK), lambda b: (b, 0, 0, 0)),
        compiler_params=SMALL,
        name="decays",
    )(jnp.transpose(cum, (1, 0, 2)), cumc, doc[:, None], docc)

    wview = w_qkv.reshape(WROWS, 3, SIDE, width)
    weights = []
    for d in range(SIDE):
        at = (z + d * (1 - 2 * c)) % SIDE
        weights.append(
            lax.dynamic_slice(wview, (0, 0, at, 0), (WROWS, 3, 1, width)).reshape(WROWS, COLS)
        )
    w, first = spread_weights(weights, (decay, kf, qf, suffix, passes, fac))
    mine = lax.dynamic_slice(tokens, ((2 * x + c) * 64, 0), (64, DEPTH))
    mine = lax.optimization_barrier((mine, *first))[0]
    group = lax.all_gather(mine, ("z", "x", "c"), axis=0, tiled=True)

    proj = call_project(place, tokens, group.reshape(SIDE, SPAN, DEPTH), w)
    proj = proj.reshape(GROUP, COLS)
    states, total = pl.pallas_call(
        block_states,
        out_shape=(
            jax.ShapeDtypeStruct((NB, HH) + square, jnp.float32),
            jax.ShapeDtypeStruct((HH,) + square, jnp.bfloat16),
        ),
        grid=(1,),
        in_specs=[
            pl.BlockSpec((GROUP, width), lambda i: (0, 1)),
            pl.BlockSpec((GROUP, width), lambda i: (0, 2)),
            vmem,
            smem,
        ],
        out_specs=(vmem, vmem),
        cost_estimate=pl.CostEstimate(flops=1 << 27, bytes_accessed=4 << 20, transcendentals=0),
        compiler_params=SMALL,
        name="states",
    )(proj, proj, kf, suffix)
    s1, s2, s3 = move_y(total, 1), move_y(total, 2), move_y(total, 3)

    def block(b):
        return (b, 0)

    qd, intra = pl.pallas_call(
        intras,
        out_shape=(
            jax.ShapeDtypeStruct((GROUP, width), jnp.bfloat16),
            jax.ShapeDtypeStruct((GROUP, width), jnp.float32),
        ),
        grid=(NB,),
        in_specs=[
            pl.BlockSpec((BLOCK, COLS), block),
            pl.BlockSpec((1, HH, BLOCK, BLOCK), lambda b: (b, 0, 0, 0)),
            pl.BlockSpec((BLOCK, HH), block),
        ],
        out_specs=(pl.BlockSpec((BLOCK, width), block), pl.BlockSpec((BLOCK, width), block)),
        cost_estimate=pl.CostEstimate(flops=1 << 30, bytes_accessed=8 << 20, transcendentals=0),
        compiler_params=SMALL,
        name="intras",
    )(proj, decay, qf)
    out = pl.pallas_call(
        inters,
        out_shape=[jax.ShapeDtypeStruct((SPAN, width), jnp.bfloat16)] * SIDE
        + [jax.ShapeDtypeStruct(summed, jnp.float32)] * SIDE,
        in_specs=[smem, vmem, vmem, vmem, smem, smem, vmem, vmem, vmem],
        out_specs=[hbm] * (2 * SIDE),
        scratch_shapes=[
            pltpu.VMEM((SIDE, SPAN, width), jnp.bfloat16),
            pltpu.VMEM((SIDE,) + summed, jnp.float32),
            pltpu.SemaphoreType.DMA((2 * SIDE,)),
        ],
        cost_estimate=pl.CostEstimate(flops=1 << 28, bytes_accessed=6 << 20, transcendentals=0),
        compiler_params=SMALL,
        name="inters",
    )(place, qd, intra, states, passes, fac, s1, s2, s3)

    pieces, part = list(out[:SIDE]), out[SIDE]
    pieces[1], pieces[2] = move_z(pieces[1], 1), move_z(pieces[2], -1)
    for i, d in enumerate((1, -1, 2)):
        part = part + move_z(out[SIDE + 1 + i], d)
    part = part + swap(part)
    part = lax.optimization_barrier((part, pieces[1], pieces[2]))[0]
    pieces[3] = move_z(pieces[3], 2)
    part = part + move_x(part, 1) + move_x(part, -1) + move_x(part, 2)
    return pl.pallas_call(
        finish,
        out_shape=jax.ShapeDtypeStruct((SPAN, SIDE * width), jnp.bfloat16),
        in_specs=[smem] + [vmem] * 6,
        out_specs=vmem,
        cost_estimate=pl.CostEstimate(flops=1 << 22, bytes_accessed=3 << 20, transcendentals=0),
        compiler_params=SMALL,
        name="finish",
    )(place, part, norm_gain.reshape(1, -1), *pieces)


def solution(mesh):
    mesh = jax.sharding.Mesh(mesh.devices.reshape(SIDE, SIDE, SIDE, 2), AXES)
    in_specs = (
        P(("y", "z"), None),
        P(("y", "z"), None, ("x", "c")),
        P(("x", "c"), None),
        P(),
        P(("x", "c")),
    )
    out_specs = P(("y", "z"), ("x", "c"))
    return jax.shard_map(
        per_device, mesh=mesh, in_specs=in_specs, out_specs=out_specs, check_vma=False
    )
```

```python
import functools

import jax
import jax.numpy as jnp
from jax import lax
from jax.experimental import pallas as pl
from jax.experimental.pallas import tpu as pltpu
from jax.sharding import PartitionSpec as P

AXES = ("y", "z", "x", "c")
HEADS = 64
HDIM = 128
BLOCK = 256
SIDE = 4
SPAN = 512
DEPTH = 6144
WROWS = 384
HH = 2
COLS = 3 * HH * HDIM
GROUP = SIDE * SPAN
NB = GROUP // BLOCK
VMEM = pltpu.CompilerParams(vmem_limit_bytes=58 * 1024 * 1024)
SMALL = pltpu.CompilerParams(vmem_limit_bytes=24 * 1024 * 1024)


def move_y(a, d):
    return lax.ppermute(a, "y", [(s, (s + d) % 4) for s in range(4)])


def move_z(a, d):
    return lax.ppermute(a, "z", [(s, (s + d) % 4) for s in range(4)])


def move_x(a, d):
    return lax.ppermute(a, "x", [(s, (s + d) % 4) for s in range(4)])


def swap(a):
    return lax.ppermute(a, "c", [(0, 1), (1, 0)])


def opposed(a, axis, d):
    perm = [(2 * s + c, 2 * ((s + d - 2 * d * c) % 4) + c) for s in range(4) for c in range(2)]
    return lax.ppermute(a, (axis, "c"), perm)


ORDER = (
    ("y00", ""),
    ("z1", ""),
    ("z3", ""),
    ("z2", ""),
    ("y10", ""),
    ("y01", "z1"),
    ("y30", "y00"),
    ("y02", "z3"),
    ("y11", ""),
    ("y31", ""),
    ("y12", ""),
    ("y20", "y11 y02 early"),
    ("y32", ""),
    ("y21", ""),
    ("y22", ""),
)


def spread_weights(weights, early):
    got = {"z0": weights[0], "early": early}
    for name, after in ORDER:
        if name[0] == "z":
            source = weights[int(name[1])]
        elif name[2] == "0":
            source = got["z" + name[1]]
        else:
            source = got["y" + name[1] + str(int(name[2]) - 1)]
        if after:
            source = lax.optimization_barrier((source, *[got[n] for n in after.split()]))[0]
        got[name] = opposed(source, name[0], int(name[1]) if name[0] == "z" else 1)
    pieces = [
        got[n] for k in range(SIDE) for n in ["z%d" % k] + ["y%d%d" % (k, i) for i in range(3)]
    ]
    return pieces, (got["z1"], got["z3"])


def along(place, axis, steps):
    return lax.rem(place[axis] + SIDE + steps * (2 * place[3] - 1), SIDE)


def silu(total):
    half = 0.5 * total
    return (half + half * jnp.tanh(half)).astype(jnp.bfloat16)


def project_own(place, x, *refs):
    wrefs = refs[: SIDE * SIDE]
    out, wout, xbuf, wfull, result, wsem, xsem, osem = refs[-8:]
    copies = [pltpu.make_async_copy(x, xbuf, xsem.at[0])]
    for k in range(SIDE):
        for i in range(SIDE):
            at = along(place, 1, i) * SIDE + along(place, 0, k)
            rows = pl.ds(pl.multiple_of(at * WROWS, WROWS), WROWS)
            n = SIDE * k + i
            copies.append(pltpu.make_async_copy(wrefs[n], wfull.at[rows], wsem.at[n]))
    for copy in copies:
        copy.start()
    for copy in copies:
        copy.wait()
    outs = [pltpu.make_async_copy(wfull, wout, osem.at[0])]
    outs[0].start()
    for m in range(0, SPAN, BLOCK):
        rows = pl.ds(m, BLOCK)
        result[rows, :] = silu(
            jnp.dot(xbuf[rows, :], wfull[...], preferred_element_type=jnp.float32)
        )
    outs.append(pltpu.make_async_copy(result, out.at[place[0]], osem.at[1]))
    outs[1].start()
    for copy in outs:
        copy.wait()


def project_others(place, x, w, own, out):
    out[0] = silu(jnp.dot(x[0], w[...], preferred_element_type=jnp.float32))


def call_project(place, tokens, group, w):
    smem = pl.BlockSpec(memory_space=pltpu.SMEM)
    hbm = pl.BlockSpec(memory_space=pl.ANY)
    shape = jax.ShapeDtypeStruct((SIDE, SPAN, COLS), jnp.bfloat16)
    whole = (DEPTH, COLS)

    def cost(count):
        return pl.CostEstimate(
            flops=2 * count * SPAN * DEPTH * COLS,
            bytes_accessed=(10 + 7 * count) << 20,
            transcendentals=0,
        )

    own, wfull = pl.pallas_call(
        project_own,
        out_shape=(shape, jax.ShapeDtypeStruct(whole, jnp.bfloat16)),
        in_specs=[smem] + [hbm] * (1 + len(w)),
        out_specs=(hbm, hbm),
        scratch_shapes=[
            pltpu.VMEM((SPAN, DEPTH), jnp.bfloat16),
            pltpu.VMEM(whole, jnp.bfloat16),
            pltpu.VMEM((SPAN, COLS), jnp.bfloat16),
            pltpu.SemaphoreType.DMA((SIDE * SIDE,)),
            pltpu.SemaphoreType.DMA((1,)),
            pltpu.SemaphoreType.DMA((2,)),
        ],
        cost_estimate=cost(1),
        compiler_params=VMEM,
        name="project_own",
    )(place, tokens, *w)
    count = SIDE - 1
    parts = SPAN // BLOCK

    def there(i, place):
        return (lax.rem(place[0] + i // parts + 1, SIDE), i % parts, 0)

    return pl.pallas_call(
        project_others,
        out_shape=shape,
        grid_spec=pltpu.PrefetchScalarGridSpec(
            num_scalar_prefetch=1,
            grid=(count * parts,),
            in_specs=[
                pl.BlockSpec((1, BLOCK, DEPTH), there),
                pl.BlockSpec(whole, lambda i, place: (0, 0), pipeline_mode=pl.Buffered(1)),
                hbm,
            ],
            out_specs=pl.BlockSpec((1, BLOCK, COLS), there),
        ),
        input_output_aliases={3: 0},
        cost_estimate=cost(count),
        compiler_params=VMEM,
        name="project_others",
    )(place, group, wfull, own)


def decays(cumr, cumc, docr, docc, out):
    row = lax.broadcasted_iota(jnp.int32, (BLOCK, BLOCK), 0)
    col = lax.broadcasted_iota(jnp.int32, (BLOCK, BLOCK), 1)
    mask = (row >= col) & (docc[...] == docr[0])
    for h in range(HH):
        diff = cumc[:, pl.ds(h, 1)] - cumr[0, pl.ds(h, 1), :]
        out[0, h] = jnp.where(mask, jnp.exp(jnp.where(mask, diff, 0.0)), 0.0)


def block_states(keys, values, kf, suffix, states, total):
    for h in range(HH):
        held = jnp.zeros((HDIM, HDIM), jnp.float32)
        for b in range(NB):
            rows = pl.ds(b * BLOCK, BLOCK)
            k = keys[rows, pl.ds(h * HDIM, HDIM)].astype(jnp.float32)
            v = values[rows, pl.ds(h * HDIM, HDIM)]
            kd = (k * kf[rows, pl.ds(h, 1)]).astype(jnp.bfloat16)
            state = lax.dot_general(
                kd, v, (((0,), (0,)), ((), ())), preferred_element_type=jnp.float32
            )
            states[b, h] = state
            held += suffix[h, b] * state
        total[h] = held.astype(jnp.bfloat16)


def intras(proj, decay, qf, qd_out, out):
    for h in range(HH):
        cols = pl.ds(h * HDIM, HDIM)
        q = proj[:, cols]
        k = proj[:, pl.ds((HH + h) * HDIM, HDIM)]
        v = proj[:, pl.ds((2 * HH + h) * HDIM, HDIM)]
        scores = lax.dot_general(
            q, k, (((1,), (1,)), ((), ())), preferred_element_type=jnp.float32
        )
        weights = (scores * decay[0, h]).astype(jnp.bfloat16)
        out[:, cols] = jnp.dot(weights, v, preferred_element_type=jnp.float32)
        qd_out[:, cols] = (q.astype(jnp.float32) * qf[:, pl.ds(h, 1)]).astype(jnp.bfloat16)


def inters(place, qd, intra, states, passes, fac, s1, s2, s3, *refs):
    outs, squares_outs = refs[:SIDE], refs[SIDE : 2 * SIDE]
    att, squares, sem = refs[2 * SIDE :]
    near = SPAN // BLOCK
    ones = jnp.ones((8, HDIM), jnp.bfloat16)
    state = [
        fac[h, 0] * s1[h].astype(jnp.float32)
        + fac[h, 1] * s2[h].astype(jnp.float32)
        + fac[h, 2] * s3[h].astype(jnp.float32)
        for h in range(HH)
    ]
    for b in range(NB):
        rows = pl.ds(b * BLOCK, BLOCK)
        sums = jnp.zeros((BLOCK, HDIM), jnp.float32)
        for h in range(HH):
            cols = pl.ds(h * HDIM, HDIM)
            value = intra[rows, cols] + jnp.dot(
                qd[rows, cols], state[h].astype(jnp.bfloat16), preferred_element_type=jnp.float32
            )
            sums += value * value
            att[b // near, pl.ds((b % near) * BLOCK, BLOCK), cols] = value.astype(jnp.bfloat16)
            state[h] = passes[h, b] * state[h] + states[b, h]
        total = jnp.zeros((8, BLOCK), jnp.float32)
        for _ in range(3):
            piece = sums.astype(jnp.bfloat16)
            sums = sums - piece.astype(jnp.float32)
            total += lax.dot_general(
                ones, piece, (((1,), (1,)), ((), ())), preferred_element_type=jnp.float32
            )
        squares[b // near, b % near] = total
    copies = []
    for i, d in enumerate((0, 1, 3, 2)):
        target = lax.rem(place[0] + d, SIDE)
        copies.append(pltpu.make_async_copy(squares.at[target], squares_outs[i], sem.at[2 * i]))
        copies.append(pltpu.make_async_copy(att.at[target], outs[i], sem.at[2 * i + 1]))
    for copy in copies:
        copy.start()
    for copy in copies:
        copy.wait()


def finish(place, total, gain, p0, p1, p2, p3, out):
    scale = lax.rsqrt(total[...] / (HEADS * HDIM) + 1e-05)
    for b in range(SPAN // BLOCK):
        rows = pl.ds(b * BLOCK, BLOCK)
        column = jnp.transpose(scale[b])[:, 0:1]
        for dz, piece in ((0, p0), (3, p1), (1, p2), (2, p3)):
            zz = lax.rem(place[0] + dz, SIDE)
            cols = pl.ds(pl.multiple_of(zz * (HH * HDIM), HH * HDIM), HH * HDIM)
            value = piece[rows, :].astype(jnp.float32) * column
            out[rows, cols] = (value * gain[0:1, cols]).astype(jnp.bfloat16)


def doc_of(points, ends):
    found = jnp.sum((points[..., None] >= ends).astype(jnp.int32), axis=-1)
    return jnp.where(points < 0, -1, found)


def per_device(tokens, w_qkv, log_decay, doc_lengths, norm_gain):
    y, z, x, c = [lax.axis_index(axis) for axis in AXES]
    place = jnp.stack([z, y, x, c]).astype(jnp.int32)

    ends = jnp.cumsum(doc_lengths)
    nblocks = GROUP * SIDE // BLOCK
    logs = lax.dynamic_slice(log_decay, (HH * z, 0), (HH, GROUP * SIDE))
    cum_all = jnp.cumsum(logs.reshape(HH, nblocks, BLOCK), axis=2)
    starts = jnp.arange(nblocks, dtype=jnp.int32) * BLOCK
    before_all = doc_of(starts - 1, ends)
    last_all = doc_of(starts + (BLOCK - 1), ends)
    pass_all = jnp.where((before_all == last_all)[None], jnp.exp(cum_all[:, :, -1]), 0.0)
    gpass = jnp.prod(pass_all.reshape(HH, SIDE, NB), axis=2)
    f1 = jnp.where(y >= 1, 1.0, 0.0) * jnp.ones((HH,), jnp.float32)
    prev1 = lax.dynamic_index_in_dim(gpass, jnp.maximum(y - 1, 0), 1, keepdims=False)
    prev2 = lax.dynamic_index_in_dim(gpass, jnp.maximum(y - 2, 0), 1, keepdims=False)
    f2 = jnp.where(y >= 2, prev1, 0.0)
    f3 = jnp.where(y >= 3, prev1 * prev2, 0.0)
    fac = jnp.stack([f1, f2, f3], axis=1)
    passes = lax.dynamic_slice_in_dim(pass_all, NB * y, NB, 1)
    suffix = jnp.concatenate(
        [jnp.cumprod(passes[:, :0:-1], axis=1)[:, ::-1], jnp.ones((HH, 1), jnp.float32)], axis=1
    )
    cum = lax.dynamic_slice_in_dim(cum_all, NB * y, NB, 1)
    before = lax.dynamic_slice_in_dim(before_all, NB * y, NB, 0)
    last = lax.dynamic_slice_in_dim(last_all, NB * y, NB, 0)
    points = GROUP * y + jnp.arange(GROUP, dtype=jnp.int32).reshape(NB, BLOCK)
    doc = doc_of(points, ends)
    qfac = jnp.where((doc == before[:, None])[None], jnp.exp(cum), 0.0)
    kfac = jnp.where((doc == last[:, None])[None], jnp.exp(cum[:, :, -1:] - cum), 0.0)
    cumc = cum.reshape(HH, GROUP).T
    qf = qfac.reshape(HH, GROUP).T
    kf = kfac.reshape(HH, GROUP).T
    docc = doc.reshape(GROUP, 1)

    smem = pl.BlockSpec(memory_space=pltpu.SMEM)
    vmem = pl.BlockSpec(memory_space=pltpu.VMEM)
    hbm = pl.BlockSpec(memory_space=pl.ANY)
    square = (HDIM, HDIM)
    width = HH * HDIM
    near = SPAN // BLOCK
    summed = (near, 8, BLOCK)
    decay = pl.pallas_call(
        decays,
        out_shape=jax.ShapeDtypeStruct((NB, HH, BLOCK, BLOCK), jnp.float32),
        grid=(NB,),
        in_specs=[
            pl.BlockSpec((1, HH, BLOCK), lambda b: (b, 0, 0)),
            pl.BlockSpec((BLOCK, HH), lambda b: (b, 0)),
            pl.BlockSpec((1, 1, BLOCK), lambda b: (b, 0, 0)),
            pl.BlockSpec((BLOCK, 1), lambda b: (b, 0)),
        ],
        out_specs=pl.BlockSpec((1, HH, BLOCK, BLOCK), lambda b: (b, 0, 0, 0)),
        compiler_params=SMALL,
        name="decays",
    )(jnp.transpose(cum, (1, 0, 2)), cumc, doc[:, None], docc)

    weights = []
    for d in range(SIDE):
        at = (z + d * (1 - 2 * c)) % SIDE
        weights.append(
            lax.dynamic_slice(w_qkv, (0, 0, at * width), (WROWS, 3, width)).reshape(WROWS, COLS)
        )
    w, first = spread_weights(weights, (decay, kf, qf, suffix, passes, fac))
    mine = lax.dynamic_slice(tokens, ((2 * x + c) * 64, 0), (64, DEPTH))
    mine = lax.optimization_barrier((mine, *first))[0]
    group = lax.all_gather(mine, ("z", "x", "c"), axis=0, tiled=True)

    proj = call_project(place, tokens, group.reshape(SIDE, SPAN, DEPTH), w)
    proj = proj.reshape(GROUP, COLS)
    states, total = pl.pallas_call(
        block_states,
        out_shape=(
            jax.ShapeDtypeStruct((NB, HH) + square, jnp.float32),
            jax.ShapeDtypeStruct((HH,) + square, jnp.bfloat16),
        ),
        grid=(1,),
        in_specs=[
            pl.BlockSpec((GROUP, width), lambda i: (0, 1)),
            pl.BlockSpec((GROUP, width), lambda i: (0, 2)),
            vmem,
            smem,
        ],
        out_specs=(vmem, vmem),
        cost_estimate=pl.CostEstimate(flops=1 << 27, bytes_accessed=4 << 20, transcendentals=0),
        compiler_params=SMALL,
        name="states",
    )(proj, proj, kf, suffix)
    s1, s2, s3 = move_y(total, 1), move_y(total, 2), move_y(total, 3)

    def block(b):
        return (b, 0)

    qd, intra = pl.pallas_call(
        intras,
        out_shape=(
            jax.ShapeDtypeStruct((GROUP, width), jnp.bfloat16),
            jax.ShapeDtypeStruct((GROUP, width), jnp.float32),
        ),
        grid=(NB,),
        in_specs=[
            pl.BlockSpec((BLOCK, COLS), block),
            pl.BlockSpec((1, HH, BLOCK, BLOCK), lambda b: (b, 0, 0, 0)),
            pl.BlockSpec((BLOCK, HH), block),
        ],
        out_specs=(pl.BlockSpec((BLOCK, width), block), pl.BlockSpec((BLOCK, width), block)),
        cost_estimate=pl.CostEstimate(flops=1 << 30, bytes_accessed=8 << 20, transcendentals=0),
        compiler_params=SMALL,
        name="intras",
    )(proj, decay, qf)
    out = pl.pallas_call(
        inters,
        out_shape=[jax.ShapeDtypeStruct((SPAN, width), jnp.bfloat16)] * SIDE
        + [jax.ShapeDtypeStruct(summed, jnp.float32)] * SIDE,
        in_specs=[smem, vmem, vmem, vmem, smem, smem, vmem, vmem, vmem],
        out_specs=[hbm] * (2 * SIDE),
        scratch_shapes=[
            pltpu.VMEM((SIDE, SPAN, width), jnp.bfloat16),
            pltpu.VMEM((SIDE,) + summed, jnp.float32),
            pltpu.SemaphoreType.DMA((2 * SIDE,)),
        ],
        cost_estimate=pl.CostEstimate(flops=1 << 28, bytes_accessed=6 << 20, transcendentals=0),
        compiler_params=SMALL,
        name="inters",
    )(place, qd, intra, states, passes, fac, s1, s2, s3)

    pieces, part = list(out[:SIDE]), out[SIDE]
    pieces[1], pieces[2] = move_z(pieces[1], 1), move_z(pieces[2], -1)
    for i, d in enumerate((1, -1, 2)):
        part = part + move_z(out[SIDE + 1 + i], d)
    part = part + swap(part)
    part = lax.optimization_barrier((part, pieces[1], pieces[2]))[0]
    pieces[3] = move_z(pieces[3], 2)
    part = part + move_x(part, 1) + move_x(part, -1) + move_x(part, 2)
    return pl.pallas_call(
        finish,
        out_shape=jax.ShapeDtypeStruct((SPAN, SIDE * width), jnp.bfloat16),
        in_specs=[smem] + [vmem] * 6,
        out_specs=vmem,
        cost_estimate=pl.CostEstimate(flops=1 << 22, bytes_accessed=3 << 20, transcendentals=0),
        compiler_params=SMALL,
        name="finish",
    )(place, part, norm_gain.reshape(1, -1), *pieces)


def solution(mesh):
    mesh = jax.sharding.Mesh(mesh.devices.reshape(SIDE, SIDE, SIDE, 2), AXES)
    in_specs = (
        P(("y", "z"), None),
        P(("y", "z"), None, ("x", "c")),
        P(("x", "c"), None),
        P(),
        P(("x", "c")),
    )
    out_specs = P(("y", "z"), ("x", "c"))
    return jax.shard_map(
        per_device, mesh=mesh, in_specs=in_specs, out_specs=out_specs, check_vma=False
    )
```

```python
import functools

import jax
import jax.numpy as jnp
from jax import lax
from jax.experimental import pallas as pl
from jax.experimental.pallas import tpu as pltpu
from jax.sharding import PartitionSpec as P

AXES = ("y", "z", "x", "c")
HEADS = 64
HDIM = 128
BLOCK = 256
SIDE = 4
SPAN = 512
DEPTH = 6144
WROWS = 384
HH = 2
COLS = 3 * HH * HDIM
GROUP = SIDE * SPAN
NB = GROUP // BLOCK
VMEM = pltpu.CompilerParams(vmem_limit_bytes=58 * 1024 * 1024)
SMALL = pltpu.CompilerParams(vmem_limit_bytes=24 * 1024 * 1024)


def move_y(a, d):
    return lax.ppermute(a, "y", [(s, s + d) for s in range(SIDE - d)])


def move_z(a, d):
    return lax.ppermute(a, "z", [(s, (s + d) % 4) for s in range(4)])


def move_x(a, d):
    return lax.ppermute(a, "x", [(s, (s + d) % 4) for s in range(4)])


def swap(a):
    return lax.ppermute(a, "c", [(0, 1), (1, 0)])


def opposed(a, axis, d):
    perm = [(2 * s + c, 2 * ((s + d - 2 * d * c) % 4) + c) for s in range(4) for c in range(2)]
    return lax.ppermute(a, (axis, "c"), perm)


ORDER = (
    ("y00", ""),
    ("z1", ""),
    ("z3", ""),
    ("z2", ""),
    ("y10", ""),
    ("y01", "z1"),
    ("y30", "y00"),
    ("y02", "z3"),
    ("y11", ""),
    ("y31", ""),
    ("y12", ""),
    ("y20", "y11 y02 early"),
    ("y32", ""),
    ("y21", ""),
    ("y22", ""),
)


def spread_weights(weights, early):
    got = {"z0": weights[0], "early": early}
    for name, after in ORDER:
        if name[0] == "z":
            source = weights[int(name[1])]
        elif name[2] == "0":
            source = got["z" + name[1]]
        else:
            source = got["y" + name[1] + str(int(name[2]) - 1)]
        if after:
            source = lax.optimization_barrier((source, *[got[n] for n in after.split()]))[0]
        got[name] = opposed(source, name[0], int(name[1]) if name[0] == "z" else 1)
    pieces = [
        got[n] for k in range(SIDE) for n in ["z%d" % k] + ["y%d%d" % (k, i) for i in range(3)]
    ]
    return pieces, (got["z1"], got["z3"])


def along(place, axis, steps):
    return lax.rem(place[axis] + SIDE + steps * (2 * place[3] - 1), SIDE)


def silu(total):
    half = 0.5 * total
    return (half + half * jnp.tanh(half)).astype(jnp.bfloat16)


def project_own(place, x, *refs):
    wrefs = refs[: SIDE * SIDE]
    out, wout, xbuf, wfull, result, wsem, xsem, osem = refs[-8:]
    copies = [pltpu.make_async_copy(x, xbuf, xsem.at[0])]
    for k in range(SIDE):
        for i in range(SIDE):
            at = along(place, 1, i) * SIDE + along(place, 0, k)
            rows = pl.ds(pl.multiple_of(at * WROWS, WROWS), WROWS)
            n = SIDE * k + i
            copies.append(pltpu.make_async_copy(wrefs[n], wfull.at[rows], wsem.at[n]))
    for copy in copies:
        copy.start()
    for copy in copies:
        copy.wait()
    outs = [pltpu.make_async_copy(wfull, wout, osem.at[0])]
    outs[0].start()
    for m in range(0, SPAN, BLOCK):
        rows = pl.ds(m, BLOCK)
        result[rows, :] = silu(
            jnp.dot(xbuf[rows, :], wfull[...], preferred_element_type=jnp.float32)
        )
    outs.append(pltpu.make_async_copy(result, out.at[place[0]], osem.at[1]))
    outs[1].start()
    for copy in outs:
        copy.wait()


def project_others(place, x, w, own, out):
    out[0] = silu(jnp.dot(x[0], w[...], preferred_element_type=jnp.float32))


def call_project(place, tokens, group, w):
    smem = pl.BlockSpec(memory_space=pltpu.SMEM)
    hbm = pl.BlockSpec(memory_space=pl.ANY)
    shape = jax.ShapeDtypeStruct((SIDE, SPAN, COLS), jnp.bfloat16)
    whole = (DEPTH, COLS)

    def cost(count):
        return pl.CostEstimate(
            flops=2 * count * SPAN * DEPTH * COLS,
            bytes_accessed=(10 + 7 * count) << 20,
            transcendentals=0,
        )

    own, wfull = pl.pallas_call(
        project_own,
        out_shape=(shape, jax.ShapeDtypeStruct(whole, jnp.bfloat16)),
        in_specs=[smem] + [hbm] * (1 + len(w)),
        out_specs=(hbm, hbm),
        scratch_shapes=[
            pltpu.VMEM((SPAN, DEPTH), jnp.bfloat16),
            pltpu.VMEM(whole, jnp.bfloat16),
            pltpu.VMEM((SPAN, COLS), jnp.bfloat16),
            pltpu.SemaphoreType.DMA((SIDE * SIDE,)),
            pltpu.SemaphoreType.DMA((1,)),
            pltpu.SemaphoreType.DMA((2,)),
        ],
        cost_estimate=cost(1),
        compiler_params=VMEM,
        name="project_own",
    )(place, tokens, *w)
    count = SIDE - 1
    parts = SPAN // BLOCK

    def there(i, place):
        return (lax.rem(place[0] + i // parts + 1, SIDE), i % parts, 0)

    return pl.pallas_call(
        project_others,
        out_shape=shape,
        grid_spec=pltpu.PrefetchScalarGridSpec(
            num_scalar_prefetch=1,
            grid=(count * parts,),
            in_specs=[
                pl.BlockSpec((1, BLOCK, DEPTH), there),
                pl.BlockSpec(whole, lambda i, place: (0, 0), pipeline_mode=pl.Buffered(1)),
                hbm,
            ],
            out_specs=pl.BlockSpec((1, BLOCK, COLS), there),
        ),
        input_output_aliases={3: 0},
        cost_estimate=cost(count),
        compiler_params=VMEM,
        name="project_others",
    )(place, group, wfull, own)


def decays(cumr, cumc, docr, docc, out):
    row = lax.broadcasted_iota(jnp.int32, (BLOCK, BLOCK), 0)
    col = lax.broadcasted_iota(jnp.int32, (BLOCK, BLOCK), 1)
    mask = (row >= col) & (docc[...] == docr[0])
    for h in range(HH):
        diff = cumc[:, pl.ds(h, 1)] - cumr[0, pl.ds(h, 1), :]
        out[0, h] = jnp.where(mask, jnp.exp(jnp.where(mask, diff, 0.0)), 0.0)


def block_states(keys, values, kf, suffix, states, total):
    for h in range(HH):
        held = jnp.zeros((HDIM, HDIM), jnp.float32)
        for b in range(NB):
            rows = pl.ds(b * BLOCK, BLOCK)
            k = keys[rows, pl.ds(h * HDIM, HDIM)].astype(jnp.float32)
            v = values[rows, pl.ds(h * HDIM, HDIM)]
            kd = (k * kf[rows, pl.ds(h, 1)]).astype(jnp.bfloat16)
            state = lax.dot_general(
                kd, v, (((0,), (0,)), ((), ())), preferred_element_type=jnp.float32
            )
            states[b, h] = state
            held += suffix[h, b] * state
        total[h] = held.astype(jnp.bfloat16)


def intras(proj, decay, qf, qd_out, out):
    for h in range(HH):
        cols = pl.ds(h * HDIM, HDIM)
        q = proj[:, cols]
        k = proj[:, pl.ds((HH + h) * HDIM, HDIM)]
        v = proj[:, pl.ds((2 * HH + h) * HDIM, HDIM)]
        scores = lax.dot_general(
            q, k, (((1,), (1,)), ((), ())), preferred_element_type=jnp.float32
        )
        weights = (scores * decay[0, h]).astype(jnp.bfloat16)
        out[:, cols] = jnp.dot(weights, v, preferred_element_type=jnp.float32)
        qd_out[:, cols] = (q.astype(jnp.float32) * qf[:, pl.ds(h, 1)]).astype(jnp.bfloat16)


def inters(place, qd, intra, states, passes, fac, s1, s2, s3, *refs):
    outs, squares_outs = refs[:SIDE], refs[SIDE : 2 * SIDE]
    att, squares, sem = refs[2 * SIDE :]
    near = SPAN // BLOCK
    ones = jnp.ones((8, HDIM), jnp.bfloat16)
    state = [
        fac[h, 0] * s1[h].astype(jnp.float32)
        + fac[h, 1] * s2[h].astype(jnp.float32)
        + fac[h, 2] * s3[h].astype(jnp.float32)
        for h in range(HH)
    ]
    for b in range(NB):
        rows = pl.ds(b * BLOCK, BLOCK)
        sums = jnp.zeros((BLOCK, HDIM), jnp.float32)
        for h in range(HH):
            cols = pl.ds(h * HDIM, HDIM)
            value = intra[rows, cols] + jnp.dot(
                qd[rows, cols], state[h].astype(jnp.bfloat16), preferred_element_type=jnp.float32
            )
            sums += value * value
            att[b // near, pl.ds((b % near) * BLOCK, BLOCK), cols] = value.astype(jnp.bfloat16)
            state[h] = passes[h, b] * state[h] + states[b, h]
        total = jnp.zeros((8, BLOCK), jnp.float32)
        for _ in range(3):
            piece = sums.astype(jnp.bfloat16)
            sums = sums - piece.astype(jnp.float32)
            total += lax.dot_general(
                ones, piece, (((1,), (1,)), ((), ())), preferred_element_type=jnp.float32
            )
        squares[b // near, b % near] = total
    copies = []
    for i, d in enumerate((0, 1, 3, 2)):
        target = lax.rem(place[0] + d, SIDE)
        copies.append(pltpu.make_async_copy(squares.at[target], squares_outs[i], sem.at[2 * i]))
        copies.append(pltpu.make_async_copy(att.at[target], outs[i], sem.at[2 * i + 1]))
    for copy in copies:
        copy.start()
    for copy in copies:
        copy.wait()


def finish(place, total, gain, p0, p1, p2, p3, out):
    scale = lax.rsqrt(total[...] / (HEADS * HDIM) + 1e-05)
    for b in range(SPAN // BLOCK):
        rows = pl.ds(b * BLOCK, BLOCK)
        column = jnp.transpose(scale[b])[:, 0:1]
        for dz, piece in ((0, p0), (3, p1), (1, p2), (2, p3)):
            zz = lax.rem(place[0] + dz, SIDE)
            cols = pl.ds(pl.multiple_of(zz * (HH * HDIM), HH * HDIM), HH * HDIM)
            value = piece[rows, :].astype(jnp.float32) * column
            out[rows, cols] = (value * gain[0:1, cols]).astype(jnp.bfloat16)


def doc_of(points, ends):
    found = jnp.sum((points[..., None] >= ends).astype(jnp.int32), axis=-1)
    return jnp.where(points < 0, -1, found)


def per_device(tokens, w_qkv, log_decay, doc_lengths, norm_gain):
    y, z, x, c = [lax.axis_index(axis) for axis in AXES]
    place = jnp.stack([z, y, x, c]).astype(jnp.int32)

    ends = jnp.cumsum(doc_lengths)
    nblocks = GROUP * SIDE // BLOCK
    logs = lax.dynamic_slice(log_decay, (HH * z, 0), (HH, GROUP * SIDE))
    cum_all = jnp.cumsum(logs.reshape(HH, nblocks, BLOCK), axis=2)
    starts = jnp.arange(nblocks, dtype=jnp.int32) * BLOCK
    before_all = doc_of(starts - 1, ends)
    last_all = doc_of(starts + (BLOCK - 1), ends)
    pass_all = jnp.where((before_all == last_all)[None], jnp.exp(cum_all[:, :, -1]), 0.0)
    gpass = jnp.prod(pass_all.reshape(HH, SIDE, NB), axis=2)
    f1 = jnp.where(y >= 1, 1.0, 0.0) * jnp.ones((HH,), jnp.float32)
    prev1 = lax.dynamic_index_in_dim(gpass, jnp.maximum(y - 1, 0), 1, keepdims=False)
    prev2 = lax.dynamic_index_in_dim(gpass, jnp.maximum(y - 2, 0), 1, keepdims=False)
    f2 = jnp.where(y >= 2, prev1, 0.0)
    f3 = jnp.where(y >= 3, prev1 * prev2, 0.0)
    fac = jnp.stack([f1, f2, f3], axis=1)
    passes = lax.dynamic_slice_in_dim(pass_all, NB * y, NB, 1)
    suffix = jnp.concatenate(
        [jnp.cumprod(passes[:, :0:-1], axis=1)[:, ::-1], jnp.ones((HH, 1), jnp.float32)], axis=1
    )
    cum = lax.dynamic_slice_in_dim(cum_all, NB * y, NB, 1)
    before = lax.dynamic_slice_in_dim(before_all, NB * y, NB, 0)
    last = lax.dynamic_slice_in_dim(last_all, NB * y, NB, 0)
    points = GROUP * y + jnp.arange(GROUP, dtype=jnp.int32).reshape(NB, BLOCK)
    doc = doc_of(points, ends)
    qfac = jnp.where((doc == before[:, None])[None], jnp.exp(cum), 0.0)
    kfac = jnp.where((doc == last[:, None])[None], jnp.exp(cum[:, :, -1:] - cum), 0.0)
    cumc = cum.reshape(HH, GROUP).T
    qf = qfac.reshape(HH, GROUP).T
    kf = kfac.reshape(HH, GROUP).T
    docc = doc.reshape(GROUP, 1)

    smem = pl.BlockSpec(memory_space=pltpu.SMEM)
    vmem = pl.BlockSpec(memory_space=pltpu.VMEM)
    hbm = pl.BlockSpec(memory_space=pl.ANY)
    square = (HDIM, HDIM)
    width = HH * HDIM
    near = SPAN // BLOCK
    summed = (near, 8, BLOCK)
    decay = pl.pallas_call(
        decays,
        out_shape=jax.ShapeDtypeStruct((NB, HH, BLOCK, BLOCK), jnp.float32),
        grid=(NB,),
        in_specs=[
            pl.BlockSpec((1, HH, BLOCK), lambda b: (b, 0, 0)),
            pl.BlockSpec((BLOCK, HH), lambda b: (b, 0)),
            pl.BlockSpec((1, 1, BLOCK), lambda b: (b, 0, 0)),
            pl.BlockSpec((BLOCK, 1), lambda b: (b, 0)),
        ],
        out_specs=pl.BlockSpec((1, HH, BLOCK, BLOCK), lambda b: (b, 0, 0, 0)),
        compiler_params=SMALL,
        name="decays",
    )(jnp.transpose(cum, (1, 0, 2)), cumc, doc[:, None], docc)

    weights = []
    for d in range(SIDE):
        at = (z + d * (1 - 2 * c)) % SIDE
        weights.append(
            lax.dynamic_slice(w_qkv, (0, 0, at * width), (WROWS, 3, width)).reshape(WROWS, COLS)
        )
    w, first = spread_weights(weights, (decay, kf, qf, suffix, passes, fac))
    mine = lax.dynamic_slice(tokens, ((2 * x + c) * 64, 0), (64, DEPTH))
    mine = lax.optimization_barrier((mine, *first))[0]
    group = lax.all_gather(mine, ("z", "x", "c"), axis=0, tiled=True)

    proj = call_project(place, tokens, group.reshape(SIDE, SPAN, DEPTH), w)
    proj = proj.reshape(GROUP, COLS)
    states, total = pl.pallas_call(
        block_states,
        out_shape=(
            jax.ShapeDtypeStruct((NB, HH) + square, jnp.float32),
            jax.ShapeDtypeStruct((HH,) + square, jnp.bfloat16),
        ),
        grid=(1,),
        in_specs=[
            pl.BlockSpec((GROUP, width), lambda i: (0, 1)),
            pl.BlockSpec((GROUP, width), lambda i: (0, 2)),
            vmem,
            smem,
        ],
        out_specs=(vmem, vmem),
        cost_estimate=pl.CostEstimate(flops=1 << 27, bytes_accessed=4 << 20, transcendentals=0),
        compiler_params=SMALL,
        name="states",
    )(proj, proj, kf, suffix)
    s1, s2, s3 = move_y(total, 1), move_y(total, 2), move_y(total, 3)

    def block(b):
        return (b, 0)

    qd, intra = pl.pallas_call(
        intras,
        out_shape=(
            jax.ShapeDtypeStruct((GROUP, width), jnp.bfloat16),
            jax.ShapeDtypeStruct((GROUP, width), jnp.float32),
        ),
        grid=(NB,),
        in_specs=[
            pl.BlockSpec((BLOCK, COLS), block),
            pl.BlockSpec((1, HH, BLOCK, BLOCK), lambda b: (b, 0, 0, 0)),
            pl.BlockSpec((BLOCK, HH), block),
        ],
        out_specs=(pl.BlockSpec((BLOCK, width), block), pl.BlockSpec((BLOCK, width), block)),
        cost_estimate=pl.CostEstimate(flops=1 << 30, bytes_accessed=8 << 20, transcendentals=0),
        compiler_params=SMALL,
        name="intras",
    )(proj, decay, qf)
    out = pl.pallas_call(
        inters,
        out_shape=[jax.ShapeDtypeStruct((SPAN, width), jnp.bfloat16)] * SIDE
        + [jax.ShapeDtypeStruct(summed, jnp.float32)] * SIDE,
        in_specs=[smem, vmem, vmem, vmem, smem, smem, vmem, vmem, vmem],
        out_specs=[hbm] * (2 * SIDE),
        scratch_shapes=[
            pltpu.VMEM((SIDE, SPAN, width), jnp.bfloat16),
            pltpu.VMEM((SIDE,) + summed, jnp.float32),
            pltpu.SemaphoreType.DMA((2 * SIDE,)),
        ],
        cost_estimate=pl.CostEstimate(flops=1 << 28, bytes_accessed=6 << 20, transcendentals=0),
        compiler_params=SMALL,
        name="inters",
    )(place, qd, intra, states, passes, fac, s1, s2, s3)

    pieces, part = list(out[:SIDE]), out[SIDE]
    pieces[1], pieces[2] = move_z(pieces[1], 1), move_z(pieces[2], -1)
    for i, d in enumerate((1, -1, 2)):
        part = part + move_z(out[SIDE + 1 + i], d)
    part = part + swap(part)
    part = lax.optimization_barrier((part, pieces[1], pieces[2]))[0]
    pieces[3] = move_z(pieces[3], 2)
    part = part + move_x(part, 1) + move_x(part, -1) + move_x(part, 2)
    return pl.pallas_call(
        finish,
        out_shape=jax.ShapeDtypeStruct((SPAN, SIDE * width), jnp.bfloat16),
        in_specs=[smem] + [vmem] * 6,
        out_specs=vmem,
        cost_estimate=pl.CostEstimate(flops=1 << 22, bytes_accessed=3 << 20, transcendentals=0),
        compiler_params=SMALL,
        name="finish",
    )(place, part, norm_gain.reshape(1, -1), *pieces)


def solution(mesh):
    mesh = jax.sharding.Mesh(mesh.devices.reshape(SIDE, SIDE, SIDE, 2), AXES)
    in_specs = (
        P(("y", "z"), None),
        P(("y", "z"), None, ("x", "c")),
        P(("x", "c"), None),
        P(),
        P(("x", "c")),
    )
    out_specs = P(("y", "z"), ("x", "c"))
    return jax.shard_map(
        per_device, mesh=mesh, in_specs=in_specs, out_specs=out_specs, check_vma=False
    )
```

```python
import functools

import jax
import jax.numpy as jnp
from jax import lax
from jax.experimental import pallas as pl
from jax.experimental.pallas import tpu as pltpu
from jax.sharding import PartitionSpec as P

AXES = ("y", "z", "x", "c")
HEADS = 64
HDIM = 128
BLOCK = 256
SIDE = 4
SPAN = 512
DEPTH = 6144
WROWS = 384
HH = 2
COLS = 3 * HH * HDIM
GROUP = SIDE * SPAN
NB = GROUP // BLOCK
VMEM = pltpu.CompilerParams(vmem_limit_bytes=58 * 1024 * 1024)
SMALL = pltpu.CompilerParams(vmem_limit_bytes=24 * 1024 * 1024)


def move_y(a, d):
    return lax.ppermute(a, "y", [(s, (s + d) % 4) for s in range(4)])


def move_z(a, d):
    return lax.ppermute(a, "z", [(s, (s + d) % 4) for s in range(4)])


def move_x(a, d):
    return lax.ppermute(a, "x", [(s, (s + d) % 4) for s in range(4)])


def swap(a):
    return lax.ppermute(a, "c", [(0, 1), (1, 0)])


def opposed(a, axis, d):
    perm = [(2 * s + c, 2 * ((s + d - 2 * d * c) % 4) + c) for s in range(4) for c in range(2)]
    return lax.ppermute(a, (axis, "c"), perm)


ORDER = (
    ("y00", ""),
    ("z1", ""),
    ("z3", ""),
    ("z2", ""),
    ("y10", ""),
    ("y01", "z1"),
    ("y30", "y00"),
    ("y02", "z3"),
    ("y11", ""),
    ("y31", ""),
    ("y12", ""),
    ("y20", "y11 y02 early"),
    ("y32", ""),
    ("y21", ""),
    ("y22", ""),
)


def spread_weights(weights, early):
    got = {"z0": weights[0], "early": early}
    weights[3] = lax.optimization_barrier((weights[3], weights[0]))[0]
    for name, after in ORDER:
        if name[0] == "z":
            source = weights[int(name[1])]
        elif name[2] == "0":
            source = got["z" + name[1]]
        else:
            source = got["y" + name[1] + str(int(name[2]) - 1)]
        if after:
            source = lax.optimization_barrier((source, *[got[n] for n in after.split()]))[0]
        got[name] = opposed(source, name[0], int(name[1]) if name[0] == "z" else 1)
    pieces = [
        got[n] for k in range(SIDE) for n in ["z%d" % k] + ["y%d%d" % (k, i) for i in range(3)]
    ]
    return pieces, (got["z1"], got["z3"])


def along(place, axis, steps):
    return lax.rem(place[axis] + SIDE + steps * (2 * place[3] - 1), SIDE)


def silu(total):
    half = 0.5 * total
    return (half + half * jnp.tanh(half)).astype(jnp.bfloat16)


def project_own(place, x, *refs):
    wrefs = refs[: SIDE * SIDE]
    out, wout, xbuf, wfull, result, wsem, xsem, osem = refs[-8:]
    copies = [pltpu.make_async_copy(x, xbuf, xsem.at[0])]
    for k in range(SIDE):
        for i in range(SIDE):
            at = along(place, 1, i) * SIDE + along(place, 0, k)
            rows = pl.ds(pl.multiple_of(at * WROWS, WROWS), WROWS)
            n = SIDE * k + i
            copies.append(pltpu.make_async_copy(wrefs[n], wfull.at[rows], wsem.at[n]))
    for copy in copies:
        copy.start()
    for copy in copies:
        copy.wait()
    outs = [pltpu.make_async_copy(wfull, wout, osem.at[0])]
    outs[0].start()
    for m in range(0, SPAN, BLOCK):
        rows = pl.ds(m, BLOCK)
        result[rows, :] = silu(
            jnp.dot(xbuf[rows, :], wfull[...], preferred_element_type=jnp.float32)
        )
    outs.append(pltpu.make_async_copy(result, out.at[place[0]], osem.at[1]))
    outs[1].start()
    for copy in outs:
        copy.wait()


def project_others(place, x, w, own, out):
    out[0] = silu(jnp.dot(x[0], w[...], preferred_element_type=jnp.float32))


def call_project(place, tokens, group, w):
    smem = pl.BlockSpec(memory_space=pltpu.SMEM)
    hbm = pl.BlockSpec(memory_space=pl.ANY)
    shape = jax.ShapeDtypeStruct((SIDE, SPAN, COLS), jnp.bfloat16)
    whole = (DEPTH, COLS)

    def cost(count):
        return pl.CostEstimate(
            flops=2 * count * SPAN * DEPTH * COLS,
            bytes_accessed=(10 + 7 * count) << 20,
            transcendentals=0,
        )

    own, wfull = pl.pallas_call(
        project_own,
        out_shape=(shape, jax.ShapeDtypeStruct(whole, jnp.bfloat16)),
        in_specs=[smem] + [hbm] * (1 + len(w)),
        out_specs=(hbm, hbm),
        scratch_shapes=[
            pltpu.VMEM((SPAN, DEPTH), jnp.bfloat16),
            pltpu.VMEM(whole, jnp.bfloat16),
            pltpu.VMEM((SPAN, COLS), jnp.bfloat16),
            pltpu.SemaphoreType.DMA((SIDE * SIDE,)),
            pltpu.SemaphoreType.DMA((1,)),
            pltpu.SemaphoreType.DMA((2,)),
        ],
        cost_estimate=cost(1),
        compiler_params=VMEM,
        name="project_own",
    )(place, tokens, *w)
    count = SIDE - 1
    parts = SPAN // BLOCK

    def there(i, place):
        return (lax.rem(place[0] + i // parts + 1, SIDE), i % parts, 0)

    return pl.pallas_call(
        project_others,
        out_shape=shape,
        grid_spec=pltpu.PrefetchScalarGridSpec(
            num_scalar_prefetch=1,
            grid=(count * parts,),
            in_specs=[
                pl.BlockSpec((1, BLOCK, DEPTH), there),
                pl.BlockSpec(whole, lambda i, place: (0, 0), pipeline_mode=pl.Buffered(1)),
                hbm,
            ],
            out_specs=pl.BlockSpec((1, BLOCK, COLS), there),
        ),
        input_output_aliases={3: 0},
        cost_estimate=cost(count),
        compiler_params=VMEM,
        name="project_others",
    )(place, group, wfull, own)


def decays(cumr, cumc, docr, docc, out):
    row = lax.broadcasted_iota(jnp.int32, (BLOCK, BLOCK), 0)
    col = lax.broadcasted_iota(jnp.int32, (BLOCK, BLOCK), 1)
    mask = (row >= col) & (docc[...] == docr[0])
    for h in range(HH):
        diff = cumc[:, pl.ds(h, 1)] - cumr[0, pl.ds(h, 1), :]
        out[0, h] = jnp.where(mask, jnp.exp(jnp.where(mask, diff, 0.0)), 0.0)


def block_states(keys, values, kf, suffix, states, total):
    for h in range(HH):
        held = jnp.zeros((HDIM, HDIM), jnp.float32)
        for b in range(NB):
            rows = pl.ds(b * BLOCK, BLOCK)
            k = keys[rows, pl.ds(h * HDIM, HDIM)].astype(jnp.float32)
            v = values[rows, pl.ds(h * HDIM, HDIM)]
            kd = (k * kf[rows, pl.ds(h, 1)]).astype(jnp.bfloat16)
            state = lax.dot_general(
                kd, v, (((0,), (0,)), ((), ())), preferred_element_type=jnp.float32
            )
            states[b, h] = state
            held += suffix[h, b] * state
        total[h] = held.astype(jnp.bfloat16)


def intras(proj, decay, qf, qd_out, out):
    for h in range(HH):
        cols = pl.ds(h * HDIM, HDIM)
        q = proj[:, cols]
        k = proj[:, pl.ds((HH + h) * HDIM, HDIM)]
        v = proj[:, pl.ds((2 * HH + h) * HDIM, HDIM)]
        scores = lax.dot_general(
            q, k, (((1,), (1,)), ((), ())), preferred_element_type=jnp.float32
        )
        weights = (scores * decay[0, h]).astype(jnp.bfloat16)
        out[:, cols] = jnp.dot(weights, v, preferred_element_type=jnp.float32)
        qd_out[:, cols] = (q.astype(jnp.float32) * qf[:, pl.ds(h, 1)]).astype(jnp.bfloat16)


def inters(place, qd, intra, states, passes, fac, s1, s2, s3, *refs):
    outs, squares_outs = refs[:SIDE], refs[SIDE : 2 * SIDE]
    att, squares, sem = refs[2 * SIDE :]
    near = SPAN // BLOCK
    ones = jnp.ones((8, HDIM), jnp.bfloat16)
    state = [
        fac[h, 0] * s1[h].astype(jnp.float32)
        + fac[h, 1] * s2[h].astype(jnp.float32)
        + fac[h, 2] * s3[h].astype(jnp.float32)
        for h in range(HH)
    ]
    for b in range(NB):
        rows = pl.ds(b * BLOCK, BLOCK)
        sums = jnp.zeros((BLOCK, HDIM), jnp.float32)
        for h in range(HH):
            cols = pl.ds(h * HDIM, HDIM)
            value = intra[rows, cols] + jnp.dot(
                qd[rows, cols], state[h].astype(jnp.bfloat16), preferred_element_type=jnp.float32
            )
            sums += value * value
            att[b // near, pl.ds((b % near) * BLOCK, BLOCK), cols] = value.astype(jnp.bfloat16)
            state[h] = passes[h, b] * state[h] + states[b, h]
        total = jnp.zeros((8, BLOCK), jnp.float32)
        for _ in range(3):
            piece = sums.astype(jnp.bfloat16)
            sums = sums - piece.astype(jnp.float32)
            total += lax.dot_general(
                ones, piece, (((1,), (1,)), ((), ())), preferred_element_type=jnp.float32
            )
        squares[b // near, b % near] = total
    copies = []
    for i, d in enumerate((0, 1, 3, 2)):
        target = lax.rem(place[0] + d, SIDE)
        copies.append(pltpu.make_async_copy(squares.at[target], squares_outs[i], sem.at[2 * i]))
        copies.append(pltpu.make_async_copy(att.at[target], outs[i], sem.at[2 * i + 1]))
    for copy in copies:
        copy.start()
    for copy in copies:
        copy.wait()


def finish(place, total, gain, p0, p1, p2, p3, out):
    scale = lax.rsqrt(total[...] / (HEADS * HDIM) + 1e-05)
    for b in range(SPAN // BLOCK):
        rows = pl.ds(b * BLOCK, BLOCK)
        column = jnp.transpose(scale[b])[:, 0:1]
        for dz, piece in ((0, p0), (3, p1), (1, p2), (2, p3)):
            zz = lax.rem(place[0] + dz, SIDE)
            cols = pl.ds(pl.multiple_of(zz * (HH * HDIM), HH * HDIM), HH * HDIM)
            value = piece[rows, :].astype(jnp.float32) * column
            out[rows, cols] = (value * gain[0:1, cols]).astype(jnp.bfloat16)


def doc_of(points, ends):
    found = jnp.sum((points[..., None] >= ends).astype(jnp.int32), axis=-1)
    return jnp.where(points < 0, -1, found)


def per_device(tokens, w_qkv, log_decay, doc_lengths, norm_gain):
    y, z, x, c = [lax.axis_index(axis) for axis in AXES]
    place = jnp.stack([z, y, x, c]).astype(jnp.int32)

    ends = jnp.cumsum(doc_lengths)
    nblocks = GROUP * SIDE // BLOCK
    logs = lax.dynamic_slice(log_decay, (HH * z, 0), (HH, GROUP * SIDE))
    cum_all = jnp.cumsum(logs.reshape(HH, nblocks, BLOCK), axis=2)
    starts = jnp.arange(nblocks, dtype=jnp.int32) * BLOCK
    before_all = doc_of(starts - 1, ends)
    last_all = doc_of(starts + (BLOCK - 1), ends)
    pass_all = jnp.where((before_all == last_all)[None], jnp.exp(cum_all[:, :, -1]), 0.0)
    gpass = jnp.prod(pass_all.reshape(HH, SIDE, NB), axis=2)
    f1 = jnp.where(y >= 1, 1.0, 0.0) * jnp.ones((HH,), jnp.float32)
    prev1 = lax.dynamic_index_in_dim(gpass, jnp.maximum(y - 1, 0), 1, keepdims=False)
    prev2 = lax.dynamic_index_in_dim(gpass, jnp.maximum(y - 2, 0), 1, keepdims=False)
    f2 = jnp.where(y >= 2, prev1, 0.0)
    f3 = jnp.where(y >= 3, prev1 * prev2, 0.0)
    fac = jnp.stack([f1, f2, f3], axis=1)
    passes = lax.dynamic_slice_in_dim(pass_all, NB * y, NB, 1)
    suffix = jnp.concatenate(
        [jnp.cumprod(passes[:, :0:-1], axis=1)[:, ::-1], jnp.ones((HH, 1), jnp.float32)], axis=1
    )
    cum = lax.dynamic_slice_in_dim(cum_all, NB * y, NB, 1)
    before = lax.dynamic_slice_in_dim(before_all, NB * y, NB, 0)
    last = lax.dynamic_slice_in_dim(last_all, NB * y, NB, 0)
    points = GROUP * y + jnp.arange(GROUP, dtype=jnp.int32).reshape(NB, BLOCK)
    doc = doc_of(points, ends)
    qfac = jnp.where((doc == before[:, None])[None], jnp.exp(cum), 0.0)
    kfac = jnp.where((doc == last[:, None])[None], jnp.exp(cum[:, :, -1:] - cum), 0.0)
    cumc = cum.reshape(HH, GROUP).T
    qf = qfac.reshape(HH, GROUP).T
    kf = kfac.reshape(HH, GROUP).T
    docc = doc.reshape(GROUP, 1)

    smem = pl.BlockSpec(memory_space=pltpu.SMEM)
    vmem = pl.BlockSpec(memory_space=pltpu.VMEM)
    hbm = pl.BlockSpec(memory_space=pl.ANY)
    square = (HDIM, HDIM)
    width = HH * HDIM
    near = SPAN // BLOCK
    summed = (near, 8, BLOCK)
    decay = pl.pallas_call(
        decays,
        out_shape=jax.ShapeDtypeStruct((NB, HH, BLOCK, BLOCK), jnp.float32),
        grid=(NB,),
        in_specs=[
            pl.BlockSpec((1, HH, BLOCK), lambda b: (b, 0, 0)),
            pl.BlockSpec((BLOCK, HH), lambda b: (b, 0)),
            pl.BlockSpec((1, 1, BLOCK), lambda b: (b, 0, 0)),
            pl.BlockSpec((BLOCK, 1), lambda b: (b, 0)),
        ],
        out_specs=pl.BlockSpec((1, HH, BLOCK, BLOCK), lambda b: (b, 0, 0, 0)),
        compiler_params=SMALL,
        name="decays",
    )(jnp.transpose(cum, (1, 0, 2)), cumc, doc[:, None], docc)

    weights = []
    for d in range(SIDE):
        at = (z + d * (1 - 2 * c)) % SIDE
        weights.append(
            lax.dynamic_slice(w_qkv, (0, 0, at * width), (WROWS, 3, width)).reshape(WROWS, COLS)
        )
    w, first = spread_weights(weights, (decay, kf, qf, suffix, passes, fac))
    mine = lax.dynamic_slice(tokens, ((2 * x + c) * 64, 0), (64, DEPTH))
    mine = lax.optimization_barrier((mine, *first))[0]
    group = lax.all_gather(mine, ("z", "x", "c"), axis=0, tiled=True)

    proj = call_project(place, tokens, group.reshape(SIDE, SPAN, DEPTH), w)
    proj = proj.reshape(GROUP, COLS)
    states, total = pl.pallas_call(
        block_states,
        out_shape=(
            jax.ShapeDtypeStruct((NB, HH) + square, jnp.float32),
            jax.ShapeDtypeStruct((HH,) + square, jnp.bfloat16),
        ),
        grid=(1,),
        in_specs=[
            pl.BlockSpec((GROUP, width), lambda i: (0, 1)),
            pl.BlockSpec((GROUP, width), lambda i: (0, 2)),
            vmem,
            smem,
        ],
        out_specs=(vmem, vmem),
        cost_estimate=pl.CostEstimate(flops=1 << 27, bytes_accessed=4 << 20, transcendentals=0),
        compiler_params=SMALL,
        name="states",
    )(proj, proj, kf, suffix)
    s1, s2, s3 = move_y(total, 1), move_y(total, 2), move_y(total, 3)

    def block(b):
        return (b, 0)

    qd, intra = pl.pallas_call(
        intras,
        out_shape=(
            jax.ShapeDtypeStruct((GROUP, width), jnp.bfloat16),
            jax.ShapeDtypeStruct((GROUP, width), jnp.float32),
        ),
        grid=(NB,),
        in_specs=[
            pl.BlockSpec((BLOCK, COLS), block),
            pl.BlockSpec((1, HH, BLOCK, BLOCK), lambda b: (b, 0, 0, 0)),
            pl.BlockSpec((BLOCK, HH), block),
        ],
        out_specs=(pl.BlockSpec((BLOCK, width), block), pl.BlockSpec((BLOCK, width), block)),
        cost_estimate=pl.CostEstimate(flops=1 << 30, bytes_accessed=8 << 20, transcendentals=0),
        compiler_params=SMALL,
        name="intras",
    )(proj, decay, qf)
    out = pl.pallas_call(
        inters,
        out_shape=[jax.ShapeDtypeStruct((SPAN, width), jnp.bfloat16)] * SIDE
        + [jax.ShapeDtypeStruct(summed, jnp.float32)] * SIDE,
        in_specs=[smem, vmem, vmem, vmem, smem, smem, vmem, vmem, vmem],
        out_specs=[hbm] * (2 * SIDE),
        scratch_shapes=[
            pltpu.VMEM((SIDE, SPAN, width), jnp.bfloat16),
            pltpu.VMEM((SIDE,) + summed, jnp.float32),
            pltpu.SemaphoreType.DMA((2 * SIDE,)),
        ],
        cost_estimate=pl.CostEstimate(flops=1 << 28, bytes_accessed=6 << 20, transcendentals=0),
        compiler_params=SMALL,
        name="inters",
    )(place, qd, intra, states, passes, fac, s1, s2, s3)

    pieces, part = list(out[:SIDE]), out[SIDE]
    pieces[1], pieces[2] = move_z(pieces[1], 1), move_z(pieces[2], -1)
    for i, d in enumerate((1, -1, 2)):
        part = part + move_z(out[SIDE + 1 + i], d)
    part = part + swap(part)
    part = lax.optimization_barrier((part, pieces[1], pieces[2]))[0]
    pieces[3] = move_z(pieces[3], 2)
    part = part + move_x(part, 1) + move_x(part, -1) + move_x(part, 2)
    return pl.pallas_call(
        finish,
        out_shape=jax.ShapeDtypeStruct((SPAN, SIDE * width), jnp.bfloat16),
        in_specs=[smem] + [vmem] * 6,
        out_specs=vmem,
        cost_estimate=pl.CostEstimate(flops=1 << 22, bytes_accessed=3 << 20, transcendentals=0),
        compiler_params=SMALL,
        name="finish",
    )(place, part, norm_gain.reshape(1, -1), *pieces)


def solution(mesh):
    mesh = jax.sharding.Mesh(mesh.devices.reshape(SIDE, SIDE, SIDE, 2), AXES)
    in_specs = (
        P(("y", "z"), None),
        P(("y", "z"), None, ("x", "c")),
        P(("x", "c"), None),
        P(),
        P(("x", "c")),
    )
    out_specs = P(("y", "z"), ("x", "c"))
    return jax.shard_map(
        per_device, mesh=mesh, in_specs=in_specs, out_specs=out_specs, check_vma=False
    )
```
